32 devices in a mesh: rows: 8 (over z, y), feat: 4 (over x, core).
Axes of the slice: x: 2, y: 2, z: 4, core: 2. Of those that a mesh axis runs over, the one named last changes fastest.
Arguments:
- features: bfloat16 [3072, 24576], P('rows', 'feat'), may hold values from -6 to 6
- targets: float32 [3072, 512], P('rows'), may hold values from -6 to 6
- block_index: int32 [3, 128], replicated, may hold values from 0 to 3071, as said below
- inverse: float32 [3, 128, 128], replicated, may hold values from -0.5 to 0.5
Outputs:
- residual: float32 [3072, 512], P('rows')
- coeffs: float32 [3072, 512], P('rows')
The draws below stay inside these ranges and needn't reach their ends.
Inputs may be any that keep to these rules, and one draw needn't show every extreme that they name: `block_index`: entries 16 * d to 16 * (d + 1) - 1 of each row are distinct examples among 384 * d to 384 * (d + 1) - 1.
All inputs are finite; a program needn't handle non-finite values.
Results may differ from the reference program's by a relative error of at most 0.0003.
Values may be sent and summed in bfloat16 or wider, within the bound.
No kernel may reach another device: no remote copies, remote signals or barrier semaphores. Data moves between devices by JAX's collectives and lax.ppermute only.
A program may use at most 64 MiB of HBM per device.

```python
import math
import jax
import jax.numpy as jnp
from jax import lax

F = 24576
K = 512
ROWS_DEV = 384
BLOCK_DEV = 16
STEPS = 3
EXAMPLES = 3072
BLOCK = 128


def draw_features(key, part):
    key = jax.random.fold_in(key, 71)
    first = jax.random.fold_in(key, 0)
    values = jnp.clip(jax.random.normal(first, (EXAMPLES, F), jnp.float32), -5.0, 5.0)
    return values.astype(jnp.bfloat16)


def draw_block_index(key, part):
    key = jax.random.fold_in(key, 72)
    groups = BLOCK // BLOCK_DEV
    keys = jax.random.split(key, STEPS * groups)
    samples = jax.vmap(lambda single: jax.random.permutation(single, ROWS_DEV)[:BLOCK_DEV])(keys)
    offsets = jnp.arange(STEPS * groups, dtype=jnp.int32) % groups * ROWS_DEV
    picked = samples.astype(jnp.int32) + offsets[:, None]
    return picked.reshape(STEPS, BLOCK).astype(jnp.int32)


def draw_inverse(key, part):
    key = jax.random.fold_in(key, 73)
    first, second = jax.random.split(key)
    diagonal = jax.random.uniform(first, (STEPS, BLOCK), jnp.float32, 0.2, 0.5)
    spread = 0.3 / math.sqrt(BLOCK)
    other = jnp.clip(jax.random.normal(second, (STEPS, BLOCK, BLOCK), jnp.float32), -4.0, 4.0) * spread
    identity = jnp.eye(BLOCK, dtype=jnp.float32)
    return other * (1.0 - identity) + diagonal[:, :, None] * identity


def block_scale(own_key, extent, pieces, low, top_value):
    factor_of = 1.0
    for position, blocks in pieces:
        heights = jax.random.uniform(jax.random.fold_in(jax.random.fold_in(own_key, 6), position), (blocks,), jnp.float32, low / len(pieces), top_value / len(pieces))
        factor_of = factor_of * jnp.repeat(jnp.exp(heights), extent[position] // blocks).reshape((-1,) + (1,) * (len(extent) - 1 - position))
    return factor_of


def noise(own_key, extent, deviation, limit, cuts=(), kind=jnp.bfloat16):
    array = deviation * jax.random.normal(own_key, extent, jnp.float32)
    if cuts:
        array = array * block_scale(own_key, extent, cuts, -0.22, 0.18)
    return jnp.clip(array, -limit, limit).astype(kind)


def setup_inputs(seed: int = 0) -> dict:
    arg_keys = jax.random.split(jax.random.key(seed), 5)
    return {
        "features": draw_features(jax.random.fold_in(arg_keys[4], 71), 0),
        "targets": noise(arg_keys[1], (EXAMPLES, K), 1.0, 6.0, ((0, 8),), jnp.float32),
        "block_index": draw_block_index(jax.random.fold_in(arg_keys[4], 71), 0),
        "inverse": draw_inverse(jax.random.fold_in(arg_keys[4], 71), 0),
    }


def reference(features, targets, block_index, inverse):
    data = features.astype(jnp.float32)
    residual = targets
    coeffs = jnp.zeros(targets.shape, jnp.float32)
    for step in range(STEPS):
        picks = block_index[step]
        block = jnp.take(data, picks, axis=0)
        gram = jnp.dot(data, block.T, precision=lax.Precision.HIGHEST, preferred_element_type=jnp.float32)
        scaled = gram / F
        kernel = scaled + scaled * scaled
        block_resid = jnp.take(residual, picks, axis=0)
        delta = jnp.dot(inverse[step], block_resid, precision=lax.Precision.HIGHEST, preferred_element_type=jnp.float32)
        residual = residual - jnp.dot(kernel, delta, precision=lax.Precision.HIGHEST, preferred_element_type=jnp.float32)
        residual = residual.at[picks].add(-1.0 * delta)
        coeffs = coeffs.at[picks].add(delta)
    return residual, coeffs
```

```python
import functools

import jax
import jax.numpy as jnp
from jax import lax
from jax.experimental import pallas as pl
from jax.experimental.pallas import tpu as pltpu
from jax.sharding import PartitionSpec as P

F = 24576
EXACT = lax.Precision.HIGHEST


def quadratic(gram):
    scaled = gram * (1.0 / F)
    return scaled + scaled * scaled


def dot_rows(left, right):
    return lax.dot_general(
        left, right, (((1,), (1,)), ((), ())), preferred_element_type=jnp.float32
    )


def exact_dot(left, right, contract=1):
    return lax.dot_general(
        left,
        right,
        (((contract,), (0,)), ((), ())),
        precision=EXACT,
        preferred_element_type=jnp.float32,
    )


def finish_kernel(steps, per, early_slots, *refs):
    if early_slots:
        early_ref, *refs = refs
    late_ref, cross_ref, same_ref, first_ref, inverse_ref, own_ref, targets_ref, resid_ref, coeff_ref = refs
    block = first_ref.shape[1]
    rows = targets_ref.shape[0]
    deltas = []
    for step in range(steps):
        delta = first_ref[step]
        if step:
            base = step * (step - 1) // 2 * block
            change = jnp.zeros_like(delta)
            for before in range(step):
                at = slice(base + before * block, base + (before + 1) * block)
                change += exact_dot(quadratic(cross_ref[:, at]) + same_ref[:, at], deltas[before])
            delta = delta - exact_dot(inverse_ref[step], change)
        deltas.append(delta)
    spread = (own_ref[...] == lax.broadcasted_iota(jnp.int32, (steps * per, rows), 1)).astype(jnp.float32)
    own = jnp.concatenate([delta[:per] for delta in deltas], axis=0)
    coeffs = exact_dot(spread, own, 0)
    coeff_ref[...] = coeffs
    resid = targets_ref[...] - coeffs
    late = quadratic(late_ref[...]).reshape(-1, steps, per, rows)
    if early_slots:
        late = jnp.concatenate(
            [quadratic(early_ref[...]).reshape(-1, steps, per, rows), late], axis=0
        )
    for step in range(steps):
        resid = resid - exact_dot(late[:, step].reshape(block, rows), deltas[step], 0)
    resid_ref[...] = resid


def by_step(array, steps, per):
    parts = array.reshape(-1, steps, per, array.shape[-1])
    return jnp.swapaxes(parts, 0, 1).reshape(steps, -1, array.shape[-1])


class Lines:
    def __init__(self):
        self.beside = [(r, r ^ 1) for r in range(8)]
        self.pair = [(r, r ^ 2) for r in range(8)]
        self.across = [(r, r ^ 4) for r in range(8)]
        self.inner = [(r, r ^ 6) for r in range(2, 6)]
        self.outer = [(2, 0), (3, 1), (4, 6), (5, 7)]
        rank = lax.axis_index("rows")
        self.feat = lax.axis_index("feat")
        z, y = rank // 2, rank % 2
        self.is_inner = (z == 1) | (z == 2)
        low = z < 2
        line = jnp.stack([z, z ^ 1, jnp.where(low, 2, 1), jnp.where(low, 3, 0)])
        self.order = (line[:, None] * 2 + jnp.stack([y, 1 - y])[None, :]).reshape(-1)

    def rows(self, array, pairs):
        return lax.ppermute(array, "rows", pairs)

    def blocks(self, own):
        near = self.rows(own, self.pair)
        mid = self.rows(own, self.inner)
        own_b = self.rows(own, self.beside)
        near, mid, own_b = lax.optimization_barrier((near, mid, own_b))
        far = self.rows(near, self.inner)
        mid_end = self.rows(mid, self.outer)
        near_b = self.rows(near, self.beside)
        far, mid_end, near_b = lax.optimization_barrier((far, mid_end, near_b))
        far_end = self.rows(far, self.outer)
        mid = jnp.where(self.is_inner, mid, mid_end)
        mid_b = self.rows(mid, self.beside)
        far_end, mid_b = lax.optimization_barrier((far_end, mid_b))
        far = jnp.where(self.is_inner, far, far_end)
        far_b = self.rows(far, self.beside)
        return [own, own_b, near, near_b, mid, mid_b], [far, far_b]

    def residuals(self, own):
        both = jnp.concatenate([own, self.rows(own, self.beside)], axis=0)
        both = jnp.concatenate([both, self.rows(both, self.pair)], axis=0)
        other = self.rows(both, self.across)
        half = other.shape[0] // 2
        other = jnp.where(self.is_inner, jnp.concatenate([other[half:], other[:half]], axis=0), other)
        both = jnp.concatenate([both, other], axis=0)
        for bit in (1, 2):
            other = lax.ppermute(both, "feat", [(f, f ^ bit) for f in range(4)])
            first = (self.feat & bit) == 0
            both = jnp.where(
                first,
                jnp.concatenate([both, other], axis=1),
                jnp.concatenate([other, both], axis=1),
            )
        return both

    def total(self, array):
        for bit in (1, 2):
            array = array + lax.ppermute(array, "feat", [(f, f ^ bit) for f in range(4)])
        return array


class Gathers:
    def __init__(self):
        size = lax.axis_size("rows")
        self.order = (lax.axis_index("rows") + jnp.arange(size)) % size

    def turn(self, own):
        every = lax.all_gather(own, "rows", axis=0, tiled=True)
        start = lax.axis_index("rows") * own.shape[0]
        return lax.dynamic_slice_in_dim(
            jnp.concatenate([every, every], axis=0), start, every.shape[0], 0
        )

    def blocks(self, own):
        return [], [self.turn(own)]

    def residuals(self, own):
        return lax.all_gather(self.turn(own), "feat", axis=1, tiled=True)

    def total(self, array):
        return lax.psum(array, "feat")


def local(features, targets, block_index, inverse):
    rank = lax.axis_index("rows")
    row_count = lax.axis_size("rows")
    feat_count = lax.axis_size("feat")
    rows_here, columns = targets.shape
    steps, block = block_index.shape
    per = block // row_count
    lined = row_count == 8 and feat_count == 4
    mover = Lines() if lined else Gathers()
    order = mover.order

    own_picks = lax.dynamic_slice_in_dim(block_index, rank * per, per, 1) - rank * rows_here
    own_picks = own_picks.reshape(-1)
    onehot = (own_picks[:, None] == jnp.arange(rows_here)[None, :]).astype(features.dtype)
    own = lax.dot_general(
        onehot, features, (((1,), (0,)), ((), ())), preferred_element_type=features.dtype
    )
    share = columns // feat_count
    own_share = jnp.take(
        lax.dynamic_slice_in_dim(targets, lax.axis_index("feat") * share, share, 1), own_picks, axis=0
    )
    first = by_step(mover.residuals(own_share), steps, per)

    place = jnp.arange(block)
    moved = jnp.repeat(order, per) * per + place % per
    swap = moved[:, None] == place[None, :]
    picks = jnp.sum(jnp.where(swap[None], block_index[:, None, :], 0), axis=2)
    swap = swap.astype(jnp.float32)
    turned = jnp.stack(
        [exact_dot(exact_dot(swap, inverse[step]), swap.T) for step in range(steps)]
    )
    first = lax.dot_general(
        turned, first, (((2,), (1,)), ((0,), (0,))), precision=EXACT, preferred_element_type=jnp.float32
    )
    same = jnp.concatenate(
        [
            (picks[step][:, None] == picks[before][None, :]).astype(jnp.float32)
            for step in range(steps)
            for before in range(step)
        ],
        axis=1,
    )

    early, late = mover.blocks(own)
    operands = []
    if early:
        operands.append(mover.total(dot_rows(jnp.concatenate(early, axis=0), features)))
    blocks = by_step(jnp.concatenate(early + late, axis=0), steps, per)
    cross = [
        dot_rows(blocks[step], blocks[:step].reshape(step * block, -1)) for step in range(1, steps)
    ]
    late = dot_rows(jnp.concatenate(late, axis=0), features)
    flat = jnp.concatenate([late.reshape(-1)] + [part.reshape(-1) for part in cross]).reshape(-1, 128)
    flat = mover.total(flat)
    late_total = flat[: late.size // 128].reshape(late.shape)
    at = late.size // 128
    cross_total = []
    for part in cross:
        cross_total.append(flat[at : at + part.size // 128].reshape(part.shape))
        at += part.size // 128
    operands += [
        late_total,
        jnp.concatenate(cross_total, axis=1),
        same,
        first,
        turned,
        own_picks[:, None],
        targets,
    ]
    out = jax.ShapeDtypeStruct(targets.shape, jnp.float32)
    vmem = pl.BlockSpec(memory_space=pltpu.VMEM)
    return pl.pallas_call(
        functools.partial(finish_kernel, steps, per, len(early)),
        out_shape=(out, out),
        in_specs=[vmem] * len(operands),
        out_specs=(vmem, vmem),
        compiler_params=pltpu.CompilerParams(vmem_limit_bytes=48 * 1024 * 1024),
    )(*operands)


def solution(mesh):
    return jax.shard_map(
        local,
        mesh=mesh,
        in_specs=(P("rows", "feat"), P("rows", None), P(), P()),
        out_specs=(P("rows", None), P("rows", None)),
        check_vma=False,
    )
```

```python
import functools
import math

import jax
import jax.numpy as jnp
from jax import lax
from jax.experimental import pallas as pl
from jax.experimental.pallas import tpu as pltpu
from jax.sharding import PartitionSpec as P

F = 24576
EXACT = lax.Precision.HIGHEST


def quadratic(gram):
    scaled = gram * (1.0 / F)
    return scaled + scaled * scaled


def dot_rows(left, right):
    return lax.dot_general(
        left, right, (((1,), (1,)), ((), ())), preferred_element_type=jnp.float32
    )


def exact_dot(left, right, contract=1):
    return lax.dot_general(
        left,
        right,
        (((contract,), (0,)), ((), ())),
        precision=EXACT,
        preferred_element_type=jnp.float32,
    )


def pairs_of(steps):
    return [(step, before) for step in range(steps) for before in range(step)]


def finish_kernel(steps, per, grams, last, *refs):
    gram_refs, refs = refs[:grams], refs[grams:]
    if last:
        last_ref, *refs = refs
    cross_ref, same_ref, first_ref, inverse_ref, own_ref, targets_ref, resid_ref, coeff_ref = refs
    block = first_ref.shape[1]
    rows = targets_ref.shape[0]
    between = {}
    for at, (step, before) in enumerate(pairs_of(steps)):
        gram = cross_ref[:, at * block : (at + 1) * block]
        if last:
            def of(one, other):
                return jnp.concatenate(
                    [
                        jnp.zeros((block - per, block), jnp.float32),
                        last_ref[one * per : (one + 1) * per, other * block : (other + 1) * block],
                    ],
                    axis=0,
                )

            column = lax.broadcasted_iota(jnp.int32, (block, block), 0) < block - per
            gram = gram + of(step, before) + jnp.where(column, of(before, step).T, 0.0)
        between[step, before] = quadratic(gram) + same_ref[:, at * block : (at + 1) * block]
    deltas = []
    for step in range(steps):
        delta = first_ref[step]
        if step:
            change = jnp.zeros_like(delta)
            for before in range(step):
                change += exact_dot(between[step, before], deltas[before])
            delta = delta - exact_dot(inverse_ref[step], change)
        deltas.append(delta)
    spread = (own_ref[...] == lax.broadcasted_iota(jnp.int32, (steps * per, rows), 1)).astype(jnp.float32)
    own = jnp.concatenate([delta[:per] for delta in deltas], axis=0)
    coeffs = exact_dot(spread, own, 0)
    coeff_ref[...] = coeffs
    resid = targets_ref[...] - coeffs
    kernel = jnp.concatenate(
        [quadratic(ref[...]).reshape(-1, steps, per, rows) for ref in gram_refs], axis=0
    )
    for step in range(steps):
        resid = resid - exact_dot(kernel[:, step].reshape(block, rows), deltas[step], 0)
    resid_ref[...] = resid


def chunks_of(columns):
    width = math.gcd(columns, 1024)
    return [slice(at, at + width) for at in range(0, columns, width)]


def pick_kernel(picks_ref, features_ref, out_ref):
    rows = features_ref.shape[0]
    onehot = picks_ref[...] == lax.broadcasted_iota(jnp.int32, (picks_ref.shape[0], rows), 1)
    onehot = onehot.astype(jnp.float32).astype(features_ref.dtype)
    out_ref[...] = jnp.dot(onehot, features_ref[...], preferred_element_type=jnp.float32).astype(
        out_ref.dtype
    )


def pick(picks, features):
    rows, columns = features.shape
    width = math.gcd(columns, 1024)
    return pl.pallas_call(
        pick_kernel,
        grid=(columns // width,),
        out_shape=jax.ShapeDtypeStruct((picks.shape[0], columns), features.dtype),
        in_specs=[
            pl.BlockSpec((picks.shape[0], 1), lambda i: (0, 0)),
            pl.BlockSpec((rows, width), lambda i: (0, i)),
        ],
        out_specs=pl.BlockSpec((picks.shape[0], width), lambda i: (0, i)),
        cost_estimate=pl.CostEstimate(
            flops=2 * picks.shape[0] * rows * columns, bytes_accessed=rows * columns * 2, transcendentals=0
        ),
    )(picks[:, None], features)


def gram_kernel(chunks, flagged, *refs):
    if flagged:
        flag_ref, *refs = refs
    *slot_refs, features_ref, out_ref = refs
    total = jnp.zeros(out_ref.shape, jnp.float32)
    for at in chunks:
        new = [ref[:, at] for ref in slot_refs]
        total = total + dot_rows(jnp.concatenate(new, axis=0), features_ref[:, at])
    out_ref[...] = total


def cross_kernel(steps, per, chunks, count, flag_ref, *refs):
    *slot_refs, other_ref, features_ref, out_ref, pair_ref = refs
    inner = flag_ref[0] == 1
    total = jnp.zeros(out_ref.shape, jnp.float32)
    pairs = [jnp.zeros((pair_ref.shape[0], pair_ref.shape[0]), jnp.float32) for _ in pairs_of(steps)]
    for at in chunks:
        slots = [ref[:, at] for ref in slot_refs]
        slots[-1] = jnp.where(inner, slots[-1], other_ref[:, at])
        total = total + dot_rows(jnp.concatenate(slots[count:], axis=0), features_ref[:, at])
        slots.append(jnp.zeros_like(slots[0]))
        step_rows = [
            jnp.concatenate([slot[step * per : (step + 1) * per] for slot in slots], axis=0)
            for step in range(steps)
        ]
        for i, (step, before) in enumerate(pairs_of(steps)):
            pairs[i] = pairs[i] + dot_rows(step_rows[step], step_rows[before])
    out_ref[...] = total
    pair_ref[...] = jnp.concatenate(pairs, axis=1)


def last_kernel(steps, per, chunks, flag_ref, *refs):
    *slot_refs, mid_ref, end_ref, inner_ref, left_ref, right_ref, features_ref, out_ref = refs
    inner = flag_ref[0] == 1
    wide = features_ref.shape[0]
    half = left_ref.shape[1]
    total = jnp.zeros((left_ref.shape[0], wide), jnp.float32)
    cross = jnp.zeros(out_ref.shape[:1] + (out_ref.shape[1] - wide,), jnp.float32)
    for at in chunks:
        if at.start < half:
            last = left_ref[:, at]
        else:
            last = right_ref[:, at.start - half : at.stop - half]
        last = jnp.where(inner, inner_ref[:, at], last)
        slots = [ref[:, at] for ref in slot_refs] + [jnp.where(inner, mid_ref[:, at], end_ref[:, at]), last]
        every = jnp.concatenate(
            [slot[step * per : (step + 1) * per] for step in range(steps) for slot in slots], axis=0
        )
        total = total + dot_rows(last, features_ref[:, at])
        cross = cross + dot_rows(last, every)
    out_ref[:, :wide] = total
    out_ref[:, wide:] = cross


VMEM = pl.BlockSpec(memory_space=pltpu.VMEM)
SMEM = pl.BlockSpec(memory_space=pltpu.SMEM)
PARAMS = pltpu.CompilerParams(vmem_limit_bytes=48 * 1024 * 1024)


def cost(shapes, columns):
    rows = sum(m * n for m, n in shapes)
    return pl.CostEstimate(flops=2 * rows * columns, bytes_accessed=4 * rows, transcendentals=0)


def by_step(array, steps, per):
    parts = array.reshape(-1, steps, per, array.shape[-1])
    return jnp.swapaxes(parts, 0, 1).reshape(steps, -1, array.shape[-1])


class Lines:
    def __init__(self):
        self.beside = [(r, r ^ 1) for r in range(8)]
        self.pair = [(r, r ^ 2) for r in range(8)]
        self.across = [(r, r ^ 4) for r in range(8)]
        self.inner = [(r, r ^ 6) for r in range(2, 6)]
        self.outer = [(2, 0), (3, 1), (4, 6), (5, 7)]
        self.ends = [(r, r ^ 1) for r in (0, 1, 6, 7)]
        rank = lax.axis_index("rows")
        self.feat = lax.axis_index("feat")
        self.is_inner = (rank >= 2) & (rank < 6)
        self.order = rank ^ jnp.arange(8)

    def rows(self, array, pairs):
        return lax.ppermute(array, "rows", pairs)

    def near(self, array, bit):
        return lax.ppermute(array, "feat", [(f, f ^ bit) for f in range(4)])

    def joined(self, array, bit):
        other = self.near(array, bit)
        return jnp.where(
            (self.feat & bit) == 0,
            jnp.concatenate([array, other], axis=1),
            jnp.concatenate([other, array], axis=1),
        )

    def run(self, own, share, features, steps, per):
        rows = features.shape[0]
        columns = features.shape[1]
        count = own.shape[0]
        chunks = chunks_of(columns)
        half = columns // 2
        flag = self.is_inner.astype(jnp.int32)[None]
        hold = lax.optimization_barrier

        pair = self.rows(own, self.pair)
        mid = self.rows(own, self.inner)
        own_b = self.rows(own, self.beside)
        share = jnp.concatenate([share, self.rows(share, self.across)], axis=0)
        pair, mid, own_b, share = hold((pair, mid, own_b, share))

        far = self.rows(pair, self.inner)
        mid_end = self.rows(mid, self.outer)
        pair_b = self.rows(pair, self.beside)
        share = jnp.concatenate([share, self.rows(share, self.pair)], axis=0)
        far, mid_end, pair_b, share = hold((far, mid_end, pair_b, share))

        third = jnp.where(self.is_inner, far, mid_end)
        third_b = self.rows(third, self.beside)
        far_end = self.rows(far, self.outer)
        last_in = self.rows(own_b, self.inner)
        share = jnp.concatenate([share, self.rows(share, self.beside)], axis=0)
        slots = [own, own_b, pair, pair_b, third]
        first_gram = pl.pallas_call(
            functools.partial(gram_kernel, chunks, False),
            out_shape=jax.ShapeDtypeStruct((len(slots) * count, rows), jnp.float32),
            in_specs=[VMEM] * (len(slots) + 1),
            out_specs=VMEM,
            compiler_params=PARAMS,
            cost_estimate=cost([(len(slots) * count, rows)], columns),
        )(*slots, features)
        first_gram = first_gram + self.near(first_gram, 1)
        third_b, far_end, last_in, share, first_gram = hold((third_b, far_end, last_in, share, first_gram))

        last_left = self.rows(far_end[:, :half], self.ends)
        last_right = self.rows(third_b[:, half:], self.outer)
        share = self.joined(share, 1)
        first_gram = first_gram + self.near(first_gram, 2)
        slots = slots + [third_b]
        block = 8 * per
        pairs = len(pairs_of(steps))
        second_gram, cross = pl.pallas_call(
            functools.partial(cross_kernel, steps, per, chunks, 5),
            out_shape=(
                jax.ShapeDtypeStruct((2 * count, rows), jnp.float32),
                jax.ShapeDtypeStruct((block, pairs * block), jnp.float32),
            ),
            in_specs=[SMEM] + [VMEM] * (len(slots) + 3),
            out_specs=(VMEM, VMEM),
            compiler_params=PARAMS,
            cost_estimate=cost([(2 * count, rows), (block, pairs * block)], columns),
        )(flag, *slots, mid, far_end, features)
        second = jnp.concatenate([second_gram.reshape(-1, 128), cross.reshape(-1, 128)], axis=0)
        second = second + self.near(second, 1)
        last_left, last_right, share, second, first_gram = hold(
            (last_left, last_right, share, second, first_gram)
        )

        share = self.joined(share, 2)
        second = second + self.near(second, 2)
        last = pl.pallas_call(
            functools.partial(last_kernel, steps, per, chunks),
            out_shape=jax.ShapeDtypeStruct((count, rows + steps * block), jnp.float32),
            in_specs=[SMEM] + [VMEM] * (len(slots) + 6),
            out_specs=VMEM,
            compiler_params=PARAMS,
            cost_estimate=cost([(count, rows + steps * block)], columns),
        )(flag, *slots, mid, far_end, last_in, last_left, last_right, features)
        last = last + self.near(last, 1)
        last = last + self.near(last, 2)
        at = second_gram.size // 128
        second_gram = second[:at].reshape(second_gram.shape)
        cross = second[at:].reshape(cross.shape)
        share = share.reshape(2, 2, 2, count, -1).transpose(2, 1, 0, 3, 4)
        return [first_gram, second_gram, last[:, :rows]], [last[:, rows:]], cross, share.reshape(8 * count, -1)


class Gathers:
    def __init__(self):
        size = lax.axis_size("rows")
        self.order = (lax.axis_index("rows") + jnp.arange(size)) % size

    def turn(self, own):
        every = lax.all_gather(own, "rows", axis=0, tiled=True)
        start = lax.axis_index("rows") * own.shape[0]
        return lax.dynamic_slice_in_dim(
            jnp.concatenate([every, every], axis=0), start, every.shape[0], 0
        )

    def run(self, own, share, features, steps, per):
        every = self.turn(own)
        blocks = by_step(every, steps, per)
        cross = jnp.concatenate(
            [dot_rows(blocks[step], blocks[before]) for step, before in pairs_of(steps)], axis=1
        )
        gram = lax.psum(dot_rows(every, features), "feat")
        share = lax.all_gather(self.turn(share), "feat", axis=1, tiled=True)
        return [gram], [], lax.psum(cross, "feat"), share


def local(features, targets, block_index, inverse):
    rank = lax.axis_index("rows")
    row_count = lax.axis_size("rows")
    feat_count = lax.axis_size("feat")
    rows_here, columns = targets.shape
    steps, block = block_index.shape
    per = block // row_count
    mover = Lines() if (row_count, feat_count) == (8, 4) else Gathers()

    own_picks = lax.dynamic_slice_in_dim(block_index, rank * per, per, 1) - rank * rows_here
    own_picks = own_picks.reshape(-1)
    own = pick(own_picks, features)
    width = columns // feat_count
    share = jnp.take(
        lax.dynamic_slice_in_dim(targets, lax.axis_index("feat") * width, width, 1), own_picks, axis=0
    )

    place = jnp.arange(block)
    moved = jnp.repeat(mover.order, per) * per + place % per
    swap = moved[:, None] == place[None, :]
    picks = jnp.sum(jnp.where(swap[None], block_index[:, None, :], 0), axis=2)
    swap = swap.astype(jnp.float32)
    turned = jnp.stack(
        [exact_dot(exact_dot(swap, inverse[step]), swap.T) for step in range(steps)]
    )
    same = jnp.concatenate(
        [
            (picks[step][:, None] == picks[before][None, :]).astype(jnp.float32)
            for step, before in pairs_of(steps)
        ],
        axis=1,
    )

    grams, last, cross, first = mover.run(own, share, features, steps, per)
    first = lax.dot_general(
        turned,
        by_step(first, steps, per),
        (((2,), (1,)), ((0,), (0,))),
        precision=EXACT,
        preferred_element_type=jnp.float32,
    )
    operands = grams + last + [cross, same, first, turned, own_picks[:, None], targets]
    out = jax.ShapeDtypeStruct(targets.shape, jnp.float32)
    return pl.pallas_call(
        functools.partial(finish_kernel, steps, per, len(grams), bool(last)),
        out_shape=(out, out),
        in_specs=[VMEM] * len(operands),
        out_specs=(VMEM, VMEM),
        compiler_params=PARAMS,
    )(*operands)


def solution(mesh):
    return jax.shard_map(
        local,
        mesh=mesh,
        in_specs=(P("rows", "feat"), P("rows", None), P(), P()),
        out_specs=(P("rows", None), P("rows", None)),
        check_vma=False,
    )
```

```python
import functools

import jax
import jax.numpy as jnp
from jax import lax
from jax.experimental import pallas as pl
from jax.experimental.pallas import tpu as pltpu
from jax.sharding import PartitionSpec as P

F = 24576
VMEM = pl.BlockSpec(memory_space=pltpu.VMEM)
SMEM = pl.BlockSpec(memory_space=pltpu.SMEM)
PARAMS = pltpu.CompilerParams(vmem_limit_bytes=24 * 1024 * 1024)


def quadratic(gram):
    scaled = gram * (1.0 / F)
    return scaled + scaled * scaled


def dot_rows(left, right):
    return lax.dot_general(
        left, right, (((1,), (1,)), ((), ())), preferred_element_type=jnp.float32
    )


def exact_dot(left, right):
    return jnp.dot(
        left, right, precision=lax.Precision.HIGHEST, preferred_element_type=jnp.float32
    )


def split(array):
    high = array.astype(jnp.bfloat16)
    return high, (array - high.astype(jnp.float32)).astype(jnp.bfloat16)


def fine_dot(left, right, contract=1):
    sides = (((contract,), (0,)), ((), ()))
    left_high, left_low = left if isinstance(left, tuple) else split(left)
    right_high, right_low = right if isinstance(right, tuple) else split(right)

    def part(one, other):
        return lax.dot_general(one, other, sides, preferred_element_type=jnp.float32)

    return part(left_high, right_high) + (part(left_high, right_low) + part(left_low, right_high))


def pairs_of(steps):
    return [(step, before) for step in range(steps) for before in range(step)]


def of_step(slots, step, per):
    return jnp.concatenate([slot[step * per : (step + 1) * per] for slot in slots], axis=0)


def by_step(array, steps, per):
    parts = array.reshape(-1, steps, per, array.shape[-1])
    return jnp.swapaxes(parts, 0, 1).reshape(steps, -1, array.shape[-1])


def cost(rows, columns):
    return pl.CostEstimate(flops=2 * rows * columns, bytes_accessed=4 * rows, transcendentals=0)


def finish_kernel(steps, per, grams, last, *refs):
    refs = list(refs)
    gram = [refs.pop(0)[...] + refs.pop(0)[...] for _ in range(grams)]
    if last:
        end = refs.pop(0)[...] + refs.pop(0)[...]
    else:
        cross = refs.pop(0)
    same_ref, first_ref, inverse_ref, own_ref, targets_ref, resid_ref, coeff_ref = refs
    block = first_ref.shape[1]
    rows = targets_ref.shape[0]
    if last:
        cross = gram[1][-block:]
        gram[1] = gram[1][:-block]
        gram.append(end[:, :rows])
        end = end[:, rows:]
        column = lax.broadcasted_iota(jnp.int32, (block, block), 0) < block - per

        def of(one, other):
            part = end[one * per : (one + 1) * per, other * block : (other + 1) * block]
            return jnp.concatenate([jnp.zeros((block - per, block), jnp.float32), part], axis=0)

    between = {}
    for at, (step, before) in enumerate(pairs_of(steps)):
        part = cross[:, at * block : (at + 1) * block]
        if last:
            part = part + of(step, before) + jnp.where(column, of(before, step).T, 0.0)
        between[step, before] = split(quadratic(part) + same_ref[:, at * block : (at + 1) * block])
    deltas = []
    for step in range(steps):
        delta = first_ref[step]
        if step:
            change = fine_dot(between[step, 0], deltas[0])
            for before in range(1, step):
                change += fine_dot(between[step, before], deltas[before])
            delta = delta - fine_dot(inverse_ref[step], change)
        deltas.append(delta if step + 1 == steps else split(delta))
    deltas[-1] = split(deltas[-1])
    kernel = jnp.concatenate([quadratic(part) for part in gram], axis=0)
    kernel = kernel.reshape(-1, steps, per, rows)
    spread = own_ref[...] == lax.broadcasted_iota(jnp.int32, (steps * per, rows), 1)
    spread = spread.astype(jnp.float32).astype(jnp.bfloat16)
    sides = (((0,), (0,)), ((), ()))
    coeffs = jnp.zeros(targets_ref.shape, jnp.float32)
    resid = targets_ref[...]
    for high_or_low in (0, 1):
        own = jnp.concatenate([delta[high_or_low][:per] for delta in deltas], axis=0)
        coeffs += lax.dot_general(spread, own, sides, preferred_element_type=jnp.float32)
    coeff_ref[...] = coeffs
    for step in range(steps):
        resid = resid - fine_dot(kernel[:, step].reshape(block, rows), deltas[step], 0)
    resid_ref[...] = resid - coeffs


def first_kernel(steps, flag_ref, mine_ref, other_ref, inverse_ref, out_ref):
    core = flag_ref[0]
    block = inverse_ref.shape[1]
    half = mine_ref.shape[1]
    for step in range(steps):
        rows = slice(step * block, (step + 1) * block)
        inverse = split(inverse_ref[step])
        mine, other = mine_ref[rows], other_ref[rows]
        left = jnp.where(core == 0, mine, other)
        right = jnp.where(core == 0, other, mine)
        out_ref[step, :, :half] = fine_dot(inverse, left)
        out_ref[step, :, half:] = fine_dot(inverse, right)


def pick_kernel(per, low, index_ref, place_ref, features_ref, targets_ref, out_ref):
    rank, core = place_ref[0], place_ref[1]
    rows, half = features_ref.shape
    steps = index_ref.shape[0]
    line = lax.broadcasted_iota(jnp.int32, (steps * per, rows), 0)
    wanted = jnp.zeros((steps * per, rows), jnp.int32)
    for step in range(steps):
        for i in range(per):
            wanted = jnp.where(line == step * per + i, index_ref[step, rank * per + i], wanted)
    chosen = wanted - rank * rows == lax.broadcasted_iota(jnp.int32, wanted.shape, 1)
    chosen = chosen.astype(jnp.float32).astype(jnp.bfloat16)

    def take(array):
        return jnp.dot(chosen, array, preferred_element_type=jnp.float32).astype(jnp.bfloat16)

    out_ref[:, :half] = take(features_ref[...])
    width = targets_ref.shape[1] // 2
    values = jnp.where(core == 0, targets_ref[:, :width], targets_ref[:, width:])
    out_ref[:, half:] = take(split(values)[low])


def pick(block_index, place, features, targets, per, side):
    rows, columns = features.shape
    half = columns // 2
    count = block_index.shape[0] * per
    wide = half + targets.shape[1] // 2
    return pl.pallas_call(
        functools.partial(pick_kernel, per, side),
        grid=(1,),
        out_shape=jax.ShapeDtypeStruct((count, wide), features.dtype),
        in_specs=[
            SMEM,
            SMEM,
            pl.BlockSpec((rows, half), lambda i: (0, side)),
            pl.BlockSpec(targets.shape, lambda i: (0, 0)),
        ],
        out_specs=pl.BlockSpec((count, wide), lambda i: (0, 0)),
        compiler_params=PARAMS,
        cost_estimate=cost(count * rows, wide),
    )(block_index, place, features, targets)


def halves(features_ref):
    half = features_ref.shape[1] // 2
    return [(0, slice(0, half), slice(0, half)), (1, slice(0, half), slice(half, 2 * half))]


def gram_kernel(*refs):
    *slot_refs, features_ref, out_ref = refs
    total = None
    for side, at, there in halves(features_ref):
        slots = jnp.concatenate([ref[:, at] for ref in slot_refs[side::2]], axis=0)
        part = dot_rows(slots, features_ref[:, there])
        total = part if total is None else total + part
    out_ref[...] = total


def cross_kernel(steps, per, count, place_ref, *refs):
    *slot_refs, features_ref, out_ref = refs
    inner = place_ref[2] == 1
    total = [None] * (1 + len(pairs_of(steps)))
    for side, at, there in halves(features_ref):
        slots = [ref[:, at] for ref in slot_refs[side::2]]
        other = slots.pop()
        slots[-1] = jnp.where(inner, slots[-1], other)
        parts = [dot_rows(jnp.concatenate(slots[count:], axis=0), features_ref[:, there])]
        slots.append(jnp.zeros_like(other))
        rows = [of_step(slots, step, per) for step in range(steps)]
        parts += [dot_rows(rows[step], rows[before]) for step, before in pairs_of(steps)]
        total = [part if sum_ is None else sum_ + part for sum_, part in zip(total, parts)]
    new = total[0].shape[0]
    out_ref[:new] = total[0]
    out_ref[new:] = jnp.concatenate(total[1:], axis=1)


def last_kernel(steps, per, place_ref, *refs):
    *slot_refs, features_ref, out_ref, first_ref = refs
    inner = place_ref[2] == 1
    total, cross, first = None, None, 0.0
    for side, at, there in halves(features_ref):
        refs = slot_refs[side::2]
        for at in (at, slice(at.stop, refs[0].shape[1])):
            slots = [ref[:, at] for ref in refs]
            last, last_inner = slots.pop(), slots.pop()
            other = slots.pop()
            slots[-1] = jnp.where(inner, slots[-1], other)
            last = jnp.where(inner, last_inner, last)
            every = [of_step(slots + [last], step, per) for step in range(steps)]
            every = jnp.concatenate(every, axis=0)
            if at.start:
                first = first + every.astype(jnp.float32)
            else:
                part, near = dot_rows(features_ref[:, there], last), dot_rows(every, last)
                total = part if total is None else total + part
                cross = near if cross is None else cross + near
    wide = features_ref.shape[0]
    out_ref[:, :wide] = total.T
    out_ref[:, wide:] = cross.T
    first_ref[...] = first


class Lines:
    def __init__(self):
        self.beside = [(r, r ^ 1) for r in range(8)]
        self.pair = [(r, r ^ 2) for r in range(8)]
        self.inner = [(r, r ^ 6) for r in range(2, 6)]
        self.outer = [(2, 0), (3, 1), (4, 6), (5, 7)]
        self.ends = [(r, r ^ 1) for r in (0, 1, 6, 7)]
        rank = lax.axis_index("rows")
        core = lax.axis_index("feat") % 2
        self.is_inner = (rank >= 2) & (rank < 6)
        self.order = rank ^ jnp.arange(8)
        self.place = jnp.stack([rank, core, self.is_inner.astype(jnp.int32)])

    def near(self, array, bit):
        return lax.ppermute(array, "feat", [(f, f ^ bit) for f in range(4)])

    def send(self, arrays, pairs):
        return [lax.ppermute(array, "rows", pairs) for array in arrays]

    def run(self, features, targets, block_index, turned, per):
        rows, columns = features.shape
        steps, block = block_index.shape
        count = steps * per
        hold = lax.optimization_barrier
        own = [pick(block_index, self.place, features, targets, per, side) for side in range(2)]

        pair = self.send(own, self.pair)
        mid = self.send(own, self.inner)
        own_b = self.send(own, self.beside)
        for side in range(2):
            pair[side], mid[side], own_b[side] = hold((pair[side], mid[side], own_b[side]))

        far = self.send(pair, self.inner)
        mid_end = self.send(mid, self.outer)
        pair_b = self.send(pair, self.beside)
        for side in range(2):
            far[side], mid_end[side], pair_b[side] = hold((far[side], mid_end[side], pair_b[side]))

        third = [jnp.where(self.is_inner, far[side], mid_end[side]) for side in range(2)]
        third_b = self.send(third, self.beside)
        far_end = self.send(far, self.outer)
        last_in = self.send(own_b, self.inner)
        slots = own + own_b + pair + pair_b + third
        gram = pl.pallas_call(
            gram_kernel,
            out_shape=jax.ShapeDtypeStruct((5 * count, rows), jnp.float32),
            in_specs=[VMEM] * (len(slots) + 1),
            out_specs=VMEM,
            compiler_params=PARAMS,
            cost_estimate=cost(5 * count * rows, columns),
        )(*slots, features)
        gram = gram + self.near(gram, 1)
        third_b[0], far_end[0], last_in[0] = hold((third_b[0], far_end[0], last_in[0]))
        third_b[1], far_end[1], last_in[1], gram = hold((third_b[1], far_end[1], last_in[1], gram))

        ends = self.send(far_end[:1], self.ends) + self.send(third_b[1:], self.outer)
        gram_near = self.near(gram, 2)
        slots = slots + third_b + mid + far_end
        second = pl.pallas_call(
            functools.partial(cross_kernel, steps, per, 5),
            out_shape=jax.ShapeDtypeStruct((2 * count + block, rows), jnp.float32),
            in_specs=[SMEM] + [VMEM] * (len(slots) + 1),
            out_specs=VMEM,
            compiler_params=PARAMS,
            cost_estimate=cost((2 * count + block) * rows, columns),
        )(self.place, *slots, features)
        second = second + self.near(second, 1)
        ends[0], ends[1], gram_near, second = hold((ends[0], ends[1], gram_near, second))

        second_near = self.near(second, 2)
        slots = slots + last_in + ends
        last, first = pl.pallas_call(
            functools.partial(last_kernel, steps, per),
            out_shape=(
                jax.ShapeDtypeStruct((count, rows + steps * block), jnp.float32),
                jax.ShapeDtypeStruct((steps * block, targets.shape[1] // 2), jnp.float32),
            ),
            in_specs=[SMEM] + [VMEM] * (len(slots) + 1),
            out_specs=(VMEM, VMEM),
            compiler_params=PARAMS,
            cost_estimate=cost(count * (rows + steps * block), columns),
        )(self.place, *slots, features)
        last, second_near = hold((last, second_near))
        last = last + self.near(last, 1)
        last_near = self.near(last, 2)
        first = pl.pallas_call(
            functools.partial(first_kernel, steps),
            out_shape=jax.ShapeDtypeStruct((steps, block, targets.shape[1]), jnp.float32),
            in_specs=[SMEM] + [VMEM] * 3,
            out_specs=VMEM,
            compiler_params=PARAMS,
            cost_estimate=cost(3 * steps * block * block, targets.shape[1]),
        )(self.place[1:2], first, self.near(first, 1), turned)
        return 2, [gram, gram_near, second, second_near, last, last_near], first


class Gathers:
    def __init__(self):
        size = lax.axis_size("rows")
        self.order = (lax.axis_index("rows") + jnp.arange(size)) % size

    def turn(self, own):
        every = lax.all_gather(own, "rows", axis=0, tiled=True)
        start = lax.axis_index("rows") * own.shape[0]
        return lax.dynamic_slice_in_dim(
            jnp.concatenate([every, every], axis=0), start, every.shape[0], 0
        )

    def run(self, features, targets, block_index, turned, per):
        steps = block_index.shape[0]
        rank = lax.axis_index("rows")
        picks = lax.dynamic_slice_in_dim(block_index, rank * per, per, 1).reshape(-1)
        picks = picks - rank * features.shape[0]
        every = self.turn(jnp.take(features, picks, axis=0))
        width = targets.shape[1] // lax.axis_size("feat")
        start = lax.axis_index("feat") * width
        share = jnp.take(lax.dynamic_slice_in_dim(targets, start, width, 1), picks, axis=0)
        share = lax.all_gather(self.turn(share), "feat", axis=1, tiled=True)
        blocks = by_step(every, steps, per)
        cross = jnp.concatenate(
            [dot_rows(blocks[step], blocks[before]) for step, before in pairs_of(steps)], axis=1
        )
        gram, cross = lax.psum((dot_rows(every, features), cross), "feat")
        first = lax.dot_general(
            turned,
            by_step(share, steps, per),
            (((2,), (1,)), ((0,), (0,))),
            precision=lax.Precision.HIGHEST,
            preferred_element_type=jnp.float32,
        )
        return 1, [gram, jnp.zeros_like(gram), cross], first


def local(features, targets, block_index, inverse):
    rank = lax.axis_index("rows")
    row_count = lax.axis_size("rows")
    rows = features.shape[0]
    steps, block = block_index.shape
    per = block // row_count
    mover = Lines() if (row_count, lax.axis_size("feat")) == (8, 4) else Gathers()

    place = jnp.arange(block)
    moved = jnp.repeat(mover.order, per) * per + place % per
    swap = moved[:, None] == place[None, :]
    picks = jnp.sum(jnp.where(swap[None], block_index[:, None, :], 0), axis=2)
    swap = swap.astype(jnp.float32)
    turned = jnp.stack([exact_dot(exact_dot(swap, inverse[step]), swap.T) for step in range(steps)])
    same = jnp.concatenate(
        [
            (picks[step][:, None] == picks[before][None, :]).astype(jnp.float32)
            for step, before in pairs_of(steps)
        ],
        axis=1,
    )
    own = picks[:, :per].reshape(-1, 1) - rank * rows

    grams, sums, first = mover.run(features, targets, block_index, turned, per)
    operands = sums + [same, first, turned, own, targets]
    out = jax.ShapeDtypeStruct(targets.shape, jnp.float32)
    return pl.pallas_call(
        functools.partial(finish_kernel, steps, per, grams, len(sums) == 6),
        out_shape=(out, out),
        in_specs=[VMEM] * len(operands),
        out_specs=(VMEM, VMEM),
        compiler_params=PARAMS,
        cost_estimate=cost(3 * rows * steps * block, targets.shape[1]),
    )(*operands)


def solution(mesh):
    return jax.shard_map(
        local,
        mesh=mesh,
        in_specs=(P("rows", "feat"), P("rows", None), P(), P()),
        out_specs=(P("rows", None), P("rows", None)),
        check_vma=False,
    )
```

```python
import functools

import jax
import jax.numpy as jnp
from jax import lax
from jax.experimental import pallas as pl
from jax.experimental.pallas import tpu as pltpu
from jax.sharding import PartitionSpec as P

F = 24576
VMEM = pl.BlockSpec(memory_space=pltpu.VMEM)
SMEM = pl.BlockSpec(memory_space=pltpu.SMEM)
HBM = pl.BlockSpec(memory_space=pltpu.HBM)
PIECES = 4
PARAMS = pltpu.CompilerParams(vmem_limit_bytes=24 * 1024 * 1024)
PICK = pltpu.CompilerParams(vmem_limit_bytes=58 * 1024 * 1024)
GRAM = pltpu.CompilerParams(vmem_limit_bytes=46 * 1024 * 1024)


def quadratic(gram):
    scaled = gram * (1.0 / F)
    return scaled + scaled * scaled


def dot_rows(left, right):
    return lax.dot_general(
        left, right, (((1,), (1,)), ((), ())), preferred_element_type=jnp.float32
    )


def exact_dot(left, right):
    return jnp.dot(
        left, right, precision=lax.Precision.HIGHEST, preferred_element_type=jnp.float32
    )


def split(array):
    high = array.astype(jnp.bfloat16)
    return high, (array - high.astype(jnp.float32)).astype(jnp.bfloat16)


def fine_dot(left, right, contract=1):
    sides = (((contract,), (0,)), ((), ()))
    left_high, left_low = left if isinstance(left, tuple) else split(left)
    right_high, right_low = right if isinstance(right, tuple) else split(right)

    def part(one, other):
        return lax.dot_general(one, other, sides, preferred_element_type=jnp.float32)

    return part(left_high, right_high) + (part(left_high, right_low) + part(left_low, right_high))


def pairs_of(steps):
    return [(step, before) for step in range(steps) for before in range(step)]


def of_step(slots, step, per):
    return jnp.concatenate([slot[step * per : (step + 1) * per] for slot in slots], axis=0)


def by_step(array, steps, per):
    parts = array.reshape(-1, steps, per, array.shape[-1])
    return jnp.swapaxes(parts, 0, 1).reshape(steps, -1, array.shape[-1])


def cost(rows, columns):
    return pl.CostEstimate(flops=2 * rows * columns, bytes_accessed=4 * rows, transcendentals=0)


def finish_kernel(steps, per, last, *refs):
    refs = list(refs)
    if last:
        high_ref, low_ref, cross_ref = refs[:3]
        end = refs[3][...] + refs[4][...]
        refs = refs[5:]
    else:
        gram_ref, cross_ref = refs[:2]
        refs = refs[2:]
    same_ref, first_ref, inverse_ref, own_ref, targets_ref, resid_ref, coeff_ref = refs
    block = first_ref.shape[1]
    rows = targets_ref.shape[0]
    if last:
        column = lax.broadcasted_iota(jnp.int32, (block, block), 0) < block - per
        end_gram = quadratic(end[:, :rows])
        end = end[:, rows:]

        def of(one, other):
            part = end[one * per : (one + 1) * per, other * block : (other + 1) * block]
            return jnp.concatenate([jnp.zeros((block - per, block), jnp.float32), part], axis=0)

    between = {}
    for at, (step, before) in enumerate(pairs_of(steps)):
        part = cross_ref[:, at * block : (at + 1) * block]
        if last:
            part = part + of(step, before) + jnp.where(column, of(before, step).T, 0.0)
        between[step, before] = split(quadratic(part) + same_ref[:, at * block : (at + 1) * block])
    deltas = []
    for step in range(steps):
        delta = first_ref[step]
        if step:
            change = fine_dot(between[step, 0], deltas[0])
            for before in range(1, step):
                change += fine_dot(between[step, before], deltas[before])
            delta = delta - fine_dot(inverse_ref[step], change)
        deltas.append(split(delta))
    spread = own_ref[...] == lax.broadcasted_iota(jnp.int32, (steps * per, rows), 1)
    spread = spread.astype(jnp.float32).astype(jnp.bfloat16)
    sides = (((0,), (0,)), ((), ()))
    coeffs = jnp.zeros(targets_ref.shape, jnp.float32)
    resid = targets_ref[...]
    for high_or_low in (0, 1):
        own = jnp.concatenate([delta[high_or_low][:per] for delta in deltas], axis=0)
        coeffs += lax.dot_general(spread, own, sides, preferred_element_type=jnp.float32)
    coeff_ref[...] = coeffs
    for step in range(steps):
        if last:
            part = split(end_gram[step * per : (step + 1) * per])
            kernel = tuple(
                jnp.concatenate([ref[step], one], axis=0) for ref, one in zip((high_ref, low_ref), part)
            )
        else:
            kernel = quadratic(gram_ref[...].reshape(-1, steps, per, rows)[:, step].reshape(block, rows))
        resid = resid - fine_dot(kernel, deltas[step], 0)
    resid_ref[...] = resid - coeffs


def ready_kernel(steps, per, place_ref, *refs):
    mine_ref, other_ref, inverse_ref, *gram_refs, first_ref, high_ref, low_ref, cross_ref = refs
    core = place_ref[1]
    block = inverse_ref.shape[1]
    half = mine_ref.shape[1]
    for step in range(steps):
        rows = slice(step * block, (step + 1) * block)
        inverse = split(inverse_ref[step])
        mine, other = mine_ref[rows], other_ref[rows]
        first_ref[step, :, :half] = fine_dot(inverse, jnp.where(core == 0, mine, other))
        first_ref[step, :, half:] = fine_dot(inverse, jnp.where(core == 0, other, mine))
    gram = gram_refs[0][...] + gram_refs[1][...]
    second = gram_refs[2][...] + gram_refs[3][...]
    cross_ref[...] = second[-block:]
    kernel = quadratic(jnp.concatenate([gram, second[:-block]], axis=0))
    kernel = kernel.reshape(-1, steps, per, kernel.shape[-1])
    for step in range(steps):
        high_ref[step], low_ref[step] = split(kernel[:, step].reshape(block - per, -1))


def pieces_of(features_ref):
    width = features_ref.shape[1] // PIECES
    return [slice(i * width, (i + 1) * width) for i in range(PIECES)]


def fetch(features_ref, held_ref, sems):
    copies = []
    for i, at in enumerate(pieces_of(features_ref)):
        copies.append(pltpu.make_async_copy(features_ref.at[:, at], held_ref.at[:, at], sems.at[i]))
        copies[-1].start()
    return copies


def held(features):
    return [pltpu.VMEM(features.shape, features.dtype), pltpu.SemaphoreType.DMA((PIECES,))]


def add(total, part):
    return part if total is None else total + part


def pick_kernel(
    per, index_hbm, place_ref, features_ref, targets_ref, out_ref, index_ref, held_targets, side_sems, held_ref, sems
):
    index = pltpu.make_async_copy(index_hbm, index_ref, side_sems.at[0])
    index.start()
    copies = fetch(features_ref, held_ref, sems)
    side = pltpu.make_async_copy(targets_ref, held_targets, side_sems.at[1])
    side.start()
    index.wait()
    rank, core = place_ref[0], place_ref[1]
    rows, columns = features_ref.shape
    steps = index_ref.shape[0]
    line = lax.broadcasted_iota(jnp.int32, (steps * per, rows), 0)
    wanted = jnp.zeros((steps * per, rows), jnp.int32)
    for step in range(steps):
        for i in range(per):
            wanted = jnp.where(line == step * per + i, index_ref[step, rank * per + i], wanted)
    chosen = wanted - rank * rows == lax.broadcasted_iota(jnp.int32, wanted.shape, 1)
    chosen = chosen.astype(jnp.float32).astype(jnp.bfloat16)

    def take(array):
        return jnp.dot(chosen, array, preferred_element_type=jnp.float32).astype(jnp.bfloat16)

    for copy, at in zip(copies, pieces_of(features_ref)):
        copy.wait()
        out_ref[:, at] = take(held_ref[:, at])
    side.wait()
    width = targets_ref.shape[1] // 2
    values = jnp.where(core == 0, held_targets[:, :width], held_targets[:, width:])
    high, low = split(values)
    out_ref[:, columns : columns + width] = take(high)
    out_ref[:, columns + width :] = take(low)


def pick(block_index, place, features, targets, per):
    count = block_index.shape[0] * per
    wide = features.shape[1] + targets.shape[1]
    return pl.pallas_call(
        functools.partial(pick_kernel, per),
        out_shape=jax.ShapeDtypeStruct((count, wide), features.dtype),
        in_specs=[HBM, SMEM, HBM, HBM],
        out_specs=VMEM,
        scratch_shapes=[
            pltpu.SMEM(block_index.shape, jnp.int32),
            pltpu.VMEM(targets.shape, jnp.float32),
            pltpu.SemaphoreType.DMA((2,)),
        ]
        + held(features),
        compiler_params=PICK,
        cost_estimate=cost(count * features.shape[0], wide),
    )(block_index, place, features, targets)


def gram_kernel(*refs):
    *slot_refs, features_ref, out_ref, held_ref, sems = refs
    total = None
    for copy, at in zip(fetch(features_ref, held_ref, sems), pieces_of(features_ref)):
        slots = jnp.concatenate([ref[:, at] for ref in slot_refs], axis=0)
        copy.wait()
        total = add(total, dot_rows(slots, held_ref[:, at]))
    out_ref[...] = total


def cross_kernel(steps, per, count, place_ref, *refs):
    *slot_refs, features_ref, out_ref, held_ref, sems = refs
    inner = place_ref[2] == 1
    total = [None] * (1 + len(pairs_of(steps)))
    copies = fetch(features_ref, held_ref, sems)
    for copy, at in zip(copies, pieces_of(features_ref)):
        slots = [ref[:, at] for ref in slot_refs]
        other = slots.pop()
        slots[-1] = jnp.where(inner, slots[-1], other)
        rows = [of_step(slots + [jnp.zeros_like(other)], step, per) for step in range(steps)]
        for i, (step, before) in enumerate(pairs_of(steps)):
            total[1 + i] = add(total[1 + i], dot_rows(rows[step], rows[before]))
        copy.wait()
        total[0] = add(total[0], dot_rows(jnp.concatenate(slots[count:], axis=0), held_ref[:, at]))
    new = total[0].shape[0]
    out_ref[:new] = total[0]
    out_ref[new:] = jnp.concatenate(total[1:], axis=1)


def last_kernel(steps, per, place_ref, *refs):
    *slot_refs, inner_ref, left_ref, right_ref, features_ref, out_ref, first_ref, held_ref, sems = refs
    inner = place_ref[2] == 1
    columns = features_ref.shape[1]
    half = left_ref.shape[1]
    copies = fetch(features_ref, held_ref, sems)

    def every(at):
        slots = [ref[:, at] for ref in slot_refs]
        other = slots.pop()
        slots[-1] = jnp.where(inner, slots[-1], other)
        if at.start < half:
            last = left_ref[:, at]
        else:
            last = right_ref[:, at.start - half : at.stop - half]
        last = jnp.where(inner, inner_ref[:, at], last)
        rows = [of_step(slots + [last], step, per) for step in range(steps)]
        return last, jnp.concatenate(rows, axis=0)

    total, cross = None, None
    for copy, at in zip(copies, pieces_of(features_ref)):
        last, rows = every(at)
        cross = add(cross, dot_rows(rows, last))
        copy.wait()
        total = add(total, dot_rows(held_ref[:, at], last))
    wide = features_ref.shape[0]
    out_ref[:, :wide] = total.T
    out_ref[:, wide:] = cross.T
    width = (inner_ref.shape[1] - columns) // 2
    high = every(slice(columns, columns + width))[1]
    low = every(slice(columns + width, columns + 2 * width))[1]
    first_ref[...] = high.astype(jnp.float32) + low.astype(jnp.float32)


class Lines:
    def __init__(self):
        self.beside = [(r, r ^ 1) for r in range(8)]
        self.pair = [(r, r ^ 2) for r in range(8)]
        self.inner = [(r, r ^ 6) for r in range(2, 6)]
        self.outer = [(2, 0), (3, 1), (4, 6), (5, 7)]
        self.ends = [(r, r ^ 1) for r in (0, 1, 6, 7)]
        rank = lax.axis_index("rows")
        core = lax.axis_index("feat") % 2
        self.is_inner = (rank >= 2) & (rank < 6)
        self.order = rank ^ jnp.arange(8)
        self.place = jnp.stack([rank, core, self.is_inner.astype(jnp.int32)])

    def near(self, array, bit):
        return lax.ppermute(array, "feat", [(f, f ^ bit) for f in range(4)])

    def send(self, array, pairs):
        return lax.ppermute(array, "rows", pairs)

    def run(self, features, targets, block_index, turned, per):
        rows, columns = features.shape
        steps, block = block_index.shape
        count = steps * per
        hold = lax.optimization_barrier
        own = pick(block_index, self.place, features, targets, per)
        half = columns // 2

        pair = self.send(own, self.pair)
        mid = self.send(own, self.inner)
        own_b = self.send(own, self.beside)
        pair, mid, own_b = hold((pair, mid, own_b))

        far = self.send(pair, self.inner)
        mid_end = self.send(mid, self.outer)
        pair_b = self.send(pair, self.beside)
        far, mid_end, pair_b = hold((far, mid_end, pair_b))

        third = jnp.where(self.is_inner, far, mid_end)
        third_b = self.send(third, self.beside)
        far_end = self.send(far, self.outer)
        last_in = self.send(own_b, self.inner)
        slots = [own, own_b, pair, pair_b, third]
        gram = pl.pallas_call(
            gram_kernel,
            out_shape=jax.ShapeDtypeStruct((5 * count, rows), jnp.float32),
            in_specs=[VMEM] * len(slots) + [HBM],
            out_specs=VMEM,
            scratch_shapes=held(features),
            compiler_params=GRAM,
            cost_estimate=cost(5 * count * rows, columns),
        )(*slots, features)
        gram = gram + self.near(gram, 1)
        third_b, far_end, last_in, gram = hold((third_b, far_end, last_in, gram))

        left = self.send(far_end[:, :half], self.ends)
        right = self.send(third_b[:, half:], self.outer)
        gram_near = self.near(gram, 2)
        slots = slots + [third_b, mid, far_end]
        second = pl.pallas_call(
            functools.partial(cross_kernel, steps, per, 5),
            out_shape=jax.ShapeDtypeStruct((2 * count + block, rows), jnp.float32),
            in_specs=[SMEM] + [VMEM] * len(slots) + [HBM],
            out_specs=VMEM,
            scratch_shapes=held(features),
            compiler_params=GRAM,
            cost_estimate=cost((2 * count + block) * rows, columns),
        )(self.place, *slots, features)
        second = second + self.near(second, 1)
        left, right, gram_near = hold((left, right, gram_near))

        second_near = self.near(second, 2)
        slots = slots + [last_in, left, right]
        last, first = pl.pallas_call(
            functools.partial(last_kernel, steps, per),
            out_shape=(
                jax.ShapeDtypeStruct((count, rows + steps * block), jnp.float32),
                jax.ShapeDtypeStruct((steps * block, targets.shape[1] // 2), jnp.float32),
            ),
            in_specs=[SMEM] + [VMEM] * len(slots) + [HBM],
            out_specs=(VMEM, VMEM),
            scratch_shapes=held(features),
            compiler_params=GRAM,
            cost_estimate=cost(count * (rows + steps * block), columns),
        )(self.place, *slots, features)
        last, second_near = hold((last, second_near))
        last = last + self.near(last, 1)
        last_near = self.near(last, 2)
        parts = (steps, block - per, rows)
        first, high, low, cross = pl.pallas_call(
            functools.partial(ready_kernel, steps, per),
            out_shape=(
                jax.ShapeDtypeStruct((steps, block, targets.shape[1]), jnp.float32),
                jax.ShapeDtypeStruct(parts, jnp.bfloat16),
                jax.ShapeDtypeStruct(parts, jnp.bfloat16),
                jax.ShapeDtypeStruct((block, rows), jnp.float32),
            ),
            in_specs=[SMEM] + [VMEM] * 7,
            out_specs=(VMEM,) * 4,
            compiler_params=PARAMS,
            cost_estimate=cost(3 * steps * block * block, targets.shape[1]),
        )(self.place, first, self.near(first, 1), turned, gram, gram_near, second, second_near)
        return [high, low, cross, last, last_near], first


class Gathers:
    def __init__(self):
        size = lax.axis_size("rows")
        self.order = (lax.axis_index("rows") + jnp.arange(size)) % size

    def turn(self, own):
        every = lax.all_gather(own, "rows", axis=0, tiled=True)
        start = lax.axis_index("rows") * own.shape[0]
        return lax.dynamic_slice_in_dim(
            jnp.concatenate([every, every], axis=0), start, every.shape[0], 0
        )

    def run(self, features, targets, block_index, turned, per):
        steps = block_index.shape[0]
        rank = lax.axis_index("rows")
        picks = lax.dynamic_slice_in_dim(block_index, rank * per, per, 1).reshape(-1)
        picks = picks - rank * features.shape[0]
        every = self.turn(jnp.take(features, picks, axis=0))
        width = targets.shape[1] // lax.axis_size("feat")
        start = lax.axis_index("feat") * width
        share = jnp.take(lax.dynamic_slice_in_dim(targets, start, width, 1), picks, axis=0)
        share = lax.all_gather(self.turn(share), "feat", axis=1, tiled=True)
        blocks = by_step(every, steps, per)
        cross = jnp.concatenate(
            [dot_rows(blocks[step], blocks[before]) for step, before in pairs_of(steps)], axis=1
        )
        gram, cross = lax.psum((dot_rows(every, features), cross), "feat")
        first = lax.dot_general(
            turned,
            by_step(share, steps, per),
            (((2,), (1,)), ((0,), (0,))),
            precision=lax.Precision.HIGHEST,
            preferred_element_type=jnp.float32,
        )
        return [gram, cross], first


def local(features, targets, block_index, inverse):
    rank = lax.axis_index("rows")
    row_count = lax.axis_size("rows")
    rows = features.shape[0]
    steps, block = block_index.shape
    per = block // row_count
    fits = rows == len(pairs_of(steps)) * block and per % 16 == 0 and features.shape[1] % (128 * PIECES) == 0
    lined = fits and (row_count, lax.axis_size("feat")) == (8, 4)
    mover = Lines() if lined else Gathers()

    place = jnp.arange(block)
    moved = jnp.repeat(mover.order, per) * per + place % per
    swap = moved[:, None] == place[None, :]
    picks = jnp.sum(jnp.where(swap[None], block_index[:, None, :], 0), axis=2)
    swap = swap.astype(jnp.float32)
    turned = jnp.stack([exact_dot(exact_dot(swap, inverse[step]), swap.T) for step in range(steps)])
    same = jnp.concatenate(
        [
            (picks[step][:, None] == picks[before][None, :]).astype(jnp.float32)
            for step, before in pairs_of(steps)
        ],
        axis=1,
    )
    own = picks[:, :per].reshape(-1, 1) - rank * rows

    sums, first = mover.run(features, targets, block_index, turned, per)
    operands = sums + [same, first, turned, own, targets]
    out = jax.ShapeDtypeStruct(targets.shape, jnp.float32)
    return pl.pallas_call(
        functools.partial(finish_kernel, steps, per, len(sums) > 2),
        out_shape=(out, out),
        in_specs=[VMEM] * len(operands),
        out_specs=(VMEM, VMEM),
        compiler_params=PARAMS,
        cost_estimate=cost(3 * rows * steps * block, targets.shape[1]),
    )(*operands)


def solution(mesh):
    return jax.shard_map(
        local,
        mesh=mesh,
        in_specs=(P("rows", "feat"), P("rows", None), P(), P()),
        out_specs=(P("rows", None), P("rows", None)),
        check_vma=False,
    )
```

```python
import functools

import jax
import jax.numpy as jnp
from jax import lax
from jax.experimental import pallas as pl
from jax.experimental.pallas import tpu as pltpu
from jax.sharding import PartitionSpec as P

F = 24576
VMEM = pl.BlockSpec(memory_space=pltpu.VMEM)
SMEM = pl.BlockSpec(memory_space=pltpu.SMEM)
HBM = pl.BlockSpec(memory_space=pltpu.HBM)
PIECES = 4
PARAMS = pltpu.CompilerParams(vmem_limit_bytes=24 * 1024 * 1024)
PICK = pltpu.CompilerParams(vmem_limit_bytes=58 * 1024 * 1024)
GRAM = pltpu.CompilerParams(vmem_limit_bytes=48 * 1024 * 1024)


def quadratic(gram):
    scaled = gram * (1.0 / F)
    return scaled + scaled * scaled


def dot_rows(left, right):
    return lax.dot_general(
        left, right, (((1,), (1,)), ((), ())), preferred_element_type=jnp.float32
    )


def exact_dot(left, right):
    return jnp.dot(
        left, right, precision=lax.Precision.HIGHEST, preferred_element_type=jnp.float32
    )


def split(array):
    high = array.astype(jnp.bfloat16)
    return high, (array - high.astype(jnp.float32)).astype(jnp.bfloat16)


def fine_dot(left, right, contract=1):
    sides = (((contract,), (0,)), ((), ()))
    left_high, left_low = left if isinstance(left, tuple) else split(left)
    right_high, right_low = right if isinstance(right, tuple) else split(right)

    def part(one, other):
        return lax.dot_general(one, other, sides, preferred_element_type=jnp.float32)

    return part(left_high, right_high) + (part(left_high, right_low) + part(left_low, right_high))


def pairs_of(steps):
    return [(step, before) for step in range(steps) for before in range(step)]


def of_step(slots, step, per):
    return jnp.concatenate([slot[step * per : (step + 1) * per] for slot in slots], axis=0)


def by_step(array, steps, per):
    parts = array.reshape(-1, steps, per, array.shape[-1])
    return jnp.swapaxes(parts, 0, 1).reshape(steps, -1, array.shape[-1])


def cost(rows, columns):
    return pl.CostEstimate(flops=2 * rows * columns, bytes_accessed=4 * rows, transcendentals=0)


def finish_kernel(steps, per, last, *refs):
    refs = list(refs)
    if last:
        place_ref, high_ref, low_ref, cross_ref, mine_ref, other_ref = refs[:6]
        refs = refs[6:]
    else:
        gram_ref, cross_ref = refs[:2]
        refs = refs[2:]
    same_ref, first_ref, inverse_ref, own_ref, targets_ref, resid_ref, coeff_ref = refs
    block = first_ref.shape[1]
    rows = targets_ref.shape[0]
    if last:
        core = place_ref[1]
        mine, other = mine_ref[...], other_ref[...]
        end_gram = quadratic(jnp.where(core == 0, mine, other))
        end = jnp.where(core == 0, other, mine)
        count = steps * per
        begun = block - end.shape[0] // steps
        column = lax.broadcasted_iota(jnp.int32, (block, block), 0) < begun

        def end_of(array, step):
            slots = [array[i : i + count] for i in range(0, array.shape[0], count)]
            return of_step(slots, step, per)

        def of(one, other):
            part = end_of(end, one)[:, other * block : (other + 1) * block]
            return jnp.concatenate([jnp.zeros((begun, block), jnp.float32), part], axis=0)

    between = {}
    for at, (step, before) in enumerate(pairs_of(steps)):
        part = cross_ref[:, at * block : (at + 1) * block]
        if last:
            part = part + of(step, before) + jnp.where(column, of(before, step).T, 0.0)
        between[step, before] = split(quadratic(part) + same_ref[:, at * block : (at + 1) * block])
    deltas = []
    for step in range(steps):
        delta = first_ref[step]
        if step:
            change = fine_dot(between[step, 0], deltas[0])
            for before in range(1, step):
                change += fine_dot(between[step, before], deltas[before])
            delta = delta - fine_dot(inverse_ref[step], change)
        deltas.append(split(delta))
    spread = own_ref[...] == lax.broadcasted_iota(jnp.int32, (steps * per, rows), 1)
    spread = spread.astype(jnp.float32).astype(jnp.bfloat16)
    sides = (((0,), (0,)), ((), ()))
    coeffs = jnp.zeros(targets_ref.shape, jnp.float32)
    resid = targets_ref[...]
    for high_or_low in (0, 1):
        own = jnp.concatenate([delta[high_or_low][:per] for delta in deltas], axis=0)
        coeffs += lax.dot_general(spread, own, sides, preferred_element_type=jnp.float32)
    coeff_ref[...] = coeffs
    for step in range(steps):
        if last:
            part = split(end_of(end_gram, step))
            kernel = tuple(
                jnp.concatenate([ref[step], one], axis=0) for ref, one in zip((high_ref, low_ref), part)
            )
        else:
            kernel = quadratic(gram_ref[...].reshape(-1, steps, per, rows)[:, step].reshape(block, rows))
        resid = resid - fine_dot(kernel, deltas[step], 0)
    resid_ref[...] = resid - coeffs


def ready_kernel(steps, per, place_ref, *refs):
    mine_ref, other_ref, inverse_ref, *gram_refs, first_ref, high_ref, low_ref, cross_ref = refs
    core = place_ref[1]
    block = inverse_ref.shape[1]
    half = mine_ref.shape[1]
    for step in range(steps):
        rows = slice(step * block, (step + 1) * block)
        inverse = split(inverse_ref[step])
        mine, other = mine_ref[rows], other_ref[rows]
        first_ref[step, :, :half] = fine_dot(inverse, jnp.where(core == 0, mine, other))
        first_ref[step, :, half:] = fine_dot(inverse, jnp.where(core == 0, other, mine))
    gram = gram_refs[0][...] + gram_refs[1][...]
    cross_ref[...] = gram[-block:]
    kernel = quadratic(gram[:-block])
    kernel = kernel.reshape(-1, steps, per, kernel.shape[-1])
    for step in range(steps):
        high_ref[step], low_ref[step] = split(kernel[:, step].reshape(high_ref.shape[1:]))


def pieces_of(features_ref):
    width = features_ref.shape[1] // PIECES
    return [slice(i * width, (i + 1) * width) for i in range(PIECES)]


def fetch(features_ref, held_ref, sems):
    copies = []
    for i, at in enumerate(pieces_of(features_ref)):
        copies.append(pltpu.make_async_copy(features_ref.at[:, at], held_ref.at[:, at], sems.at[i]))
        copies[-1].start()
    return copies


def held(features):
    return [pltpu.VMEM(features.shape, features.dtype), pltpu.SemaphoreType.DMA((PIECES,))]


def add(total, part):
    return part if total is None else total + part


def pick_kernel(
    per, index_hbm, place_ref, features_ref, targets_ref, out_ref, index_ref, held_targets, side_sems, held_ref, sems
):
    index = pltpu.make_async_copy(index_hbm, index_ref, side_sems.at[0])
    index.start()
    side = pltpu.make_async_copy(targets_ref, held_targets, side_sems.at[1])
    side.start()
    copies = fetch(features_ref, held_ref, sems)
    index.wait()
    rank, core = place_ref[0], place_ref[1]
    rows, columns = features_ref.shape
    steps = index_ref.shape[0]
    line = lax.broadcasted_iota(jnp.int32, (steps * per, rows), 0)
    wanted = jnp.zeros((steps * per, rows), jnp.int32)
    for step in range(steps):
        for i in range(per):
            wanted = jnp.where(line == step * per + i, index_ref[step, rank * per + i], wanted)
    chosen = wanted - rank * rows == lax.broadcasted_iota(jnp.int32, wanted.shape, 1)
    chosen = chosen.astype(jnp.float32).astype(jnp.bfloat16)

    def take(array):
        return jnp.dot(chosen, array, preferred_element_type=jnp.float32).astype(jnp.bfloat16)

    side.wait()
    width = targets_ref.shape[1] // 2
    values = jnp.where(core == 0, held_targets[:, :width], held_targets[:, width:])
    high, low = split(values)
    out_ref[:, columns : columns + width] = take(high)
    out_ref[:, columns + width :] = take(low)
    for copy, at in zip(copies, pieces_of(features_ref)):
        copy.wait()
        out_ref[:, at] = take(held_ref[:, at])


def pick(block_index, place, features, targets, per):
    count = block_index.shape[0] * per
    wide = features.shape[1] + targets.shape[1]
    return pl.pallas_call(
        functools.partial(pick_kernel, per),
        out_shape=jax.ShapeDtypeStruct((count, wide), features.dtype),
        in_specs=[HBM, SMEM, HBM, HBM],
        out_specs=VMEM,
        scratch_shapes=[
            pltpu.SMEM(block_index.shape, jnp.int32),
            pltpu.VMEM(targets.shape, jnp.float32),
            pltpu.SemaphoreType.DMA((2,)),
        ]
        + held(features),
        compiler_params=PICK,
        cost_estimate=cost(count * features.shape[0], wide),
    )(block_index, place, features, targets)


def gram_kernel(steps, per, missing, *refs):
    *slot_refs, features_ref, out_ref, held_ref, sems = refs
    copies = fetch(features_ref, held_ref, sems)
    total = [None] * (1 + len(pairs_of(steps)))
    for at in pieces_of(features_ref):
        slots = [ref[:, at] for ref in slot_refs]
        slots += [jnp.zeros_like(slots[0])] * missing
        rows = [of_step(slots, step, per) for step in range(steps)]
        for i, (step, before) in enumerate(pairs_of(steps)):
            total[1 + i] = add(total[1 + i], dot_rows(rows[step], rows[before]))
    for copy, at in zip(copies, pieces_of(features_ref)):
        slots = jnp.concatenate([ref[:, at] for ref in slot_refs], axis=0)
        copy.wait()
        total[0] = add(total[0], dot_rows(slots, held_ref[:, at]))
    new = total[0].shape[0]
    out_ref[:new] = total[0]
    out_ref[new:] = jnp.concatenate(total[1:], axis=1)


def last_kernel(steps, per, begun, place_ref, *refs):
    *slot_refs, inner_ref, left_ref, right_ref, features_ref = refs[:-5]
    keep_ref, send_ref, first_ref, held_ref, sems = refs[-5:]
    core = place_ref[1]
    inner = place_ref[2] == 1
    columns = features_ref.shape[1]
    half = left_ref.shape[1]
    copies = fetch(features_ref, held_ref, sems)

    def slots_at(at):
        slots = [ref[:, at] for ref in slot_refs]
        other = slots.pop()
        slots[-1] = jnp.where(inner, slots[-1], other)
        if at.start < half:
            last = left_ref[:, at]
        else:
            last = right_ref[:, at.start - half : at.stop - half]
        return slots + [jnp.where(inner, inner_ref[:, at], last)]

    def every(slots):
        return jnp.concatenate([of_step(slots, step, per) for step in range(steps)], axis=0)

    total, cross = None, None
    for at in pieces_of(features_ref):
        slots = slots_at(at)
        cross = add(cross, dot_rows(every(slots), jnp.concatenate(slots[begun:], axis=0)))
    for copy, at in zip(copies, pieces_of(features_ref)):
        new = jnp.concatenate(slots_at(at)[begun:], axis=0)
        copy.wait()
        total = add(total, dot_rows(held_ref[:, at], new))
    total, cross = total.T, cross.T
    keep_ref[...] = jnp.where(core == 0, total, cross)
    send_ref[...] = jnp.where(core == 0, cross, total)
    width = (inner_ref.shape[1] - columns) // 2
    high = every(slots_at(slice(columns, columns + width)))
    low = every(slots_at(slice(columns + width, columns + 2 * width)))
    first_ref[...] = high.astype(jnp.float32) + low.astype(jnp.float32)


class Lines:
    def __init__(self):
        self.beside = [(r, r ^ 1) for r in range(8)]
        self.pair = [(r, r ^ 2) for r in range(8)]
        self.inner = [(r, r ^ 6) for r in range(2, 6)]
        self.outer = [(2, 0), (3, 1), (4, 6), (5, 7)]
        self.ends = [(r, r ^ 1) for r in (0, 1, 6, 7)]
        rank = lax.axis_index("rows")
        core = lax.axis_index("feat") % 2
        self.is_inner = (rank >= 2) & (rank < 6)
        self.order = rank ^ jnp.arange(8)
        self.place = jnp.stack([rank, core, self.is_inner.astype(jnp.int32)])

    def near(self, array, bit):
        return lax.ppermute(array, "feat", [(f, f ^ bit) for f in range(4)])

    def send(self, array, pairs):
        return lax.ppermute(array, "rows", pairs)

    def run(self, features, targets, block_index, turned, per):
        rows, columns = features.shape
        steps, block = block_index.shape
        count = steps * per
        hold = lax.optimization_barrier
        own = pick(block_index, self.place, features, targets, per)
        half = columns // 2

        pair = self.send(own, self.pair)
        mid = self.send(own, self.inner)
        own_b = self.send(own, self.beside)
        pair, mid, own_b = hold((pair, mid, own_b))

        far = self.send(pair, self.inner)
        mid_end = self.send(mid, self.outer)
        pair_b = self.send(pair, self.beside)
        far, mid_end, pair_b, own_b = hold((far, mid_end, pair_b, own_b))

        third = jnp.where(self.is_inner, far, mid_end)
        third_b = self.send(third, self.beside)
        far_end = self.send(far, self.outer)
        last_in = self.send(own_b, self.inner)
        slots = [own, own_b, pair, pair_b, third]
        begun = len(slots)
        gram = pl.pallas_call(
            functools.partial(gram_kernel, steps, per, 8 - begun),
            out_shape=jax.ShapeDtypeStruct((begun * count + block, rows), jnp.float32),
            in_specs=[VMEM] * begun + [HBM],
            out_specs=VMEM,
            scratch_shapes=held(features),
            compiler_params=GRAM,
            cost_estimate=cost((begun * count + block) * rows, columns),
        )(*slots, features)
        gram = gram + self.near(gram, 1)
        third_b, far_end, last_in, gram = hold((third_b, far_end, last_in, gram))

        left = self.send(far_end[:, :half], self.ends)
        right = self.send(third_b[:, half:], self.outer)
        gram_near = self.near(gram, 2)
        left, right, gram_near = hold((left, right, gram_near))

        slots = slots + [third_b, mid, far_end, last_in, left, right]
        end = jax.ShapeDtypeStruct(((8 - begun) * count, rows), jnp.float32)
        keep, given, first = pl.pallas_call(
            functools.partial(last_kernel, steps, per, begun),
            out_shape=(
                end,
                end,
                jax.ShapeDtypeStruct((steps * block, targets.shape[1] // 2), jnp.float32),
            ),
            in_specs=[SMEM] + [VMEM] * len(slots) + [HBM],
            out_specs=(VMEM,) * 3,
            scratch_shapes=held(features),
            compiler_params=GRAM,
            cost_estimate=cost((8 - begun) * count * (rows + steps * block), columns),
        )(self.place, *slots, features)
        keep = keep + self.near(given, 1)
        keep = keep + self.near(keep, 2)
        parts = (steps, begun * per, rows)
        first, high, low, cross = pl.pallas_call(
            functools.partial(ready_kernel, steps, per),
            out_shape=(
                jax.ShapeDtypeStruct((steps, block, targets.shape[1]), jnp.float32),
                jax.ShapeDtypeStruct(parts, jnp.bfloat16),
                jax.ShapeDtypeStruct(parts, jnp.bfloat16),
                jax.ShapeDtypeStruct((block, rows), jnp.float32),
            ),
            in_specs=[SMEM] + [VMEM] * 5,
            out_specs=(VMEM,) * 4,
            compiler_params=PARAMS,
            cost_estimate=cost(3 * steps * block * block, targets.shape[1]),
        )(self.place, first, self.near(first, 1), turned, gram, gram_near)
        return [self.place, high, low, cross, keep, self.near(keep, 1)], first


class Gathers:
    def __init__(self):
        size = lax.axis_size("rows")
        self.order = (lax.axis_index("rows") + jnp.arange(size)) % size

    def turn(self, own):
        every = lax.all_gather(own, "rows", axis=0, tiled=True)
        start = lax.axis_index("rows") * own.shape[0]
        return lax.dynamic_slice_in_dim(
            jnp.concatenate([every, every], axis=0), start, every.shape[0], 0
        )

    def run(self, features, targets, block_index, turned, per):
        steps = block_index.shape[0]
        rank = lax.axis_index("rows")
        picks = lax.dynamic_slice_in_dim(block_index, rank * per, per, 1).reshape(-1)
        picks = picks - rank * features.shape[0]
        every = self.turn(jnp.take(features, picks, axis=0))
        width = targets.shape[1] // lax.axis_size("feat")
        start = lax.axis_index("feat") * width
        share = jnp.take(lax.dynamic_slice_in_dim(targets, start, width, 1), picks, axis=0)
        share = lax.all_gather(self.turn(share), "feat", axis=1, tiled=True)
        blocks = by_step(every, steps, per)
        cross = jnp.concatenate(
            [dot_rows(blocks[step], blocks[before]) for step, before in pairs_of(steps)], axis=1
        )
        gram, cross = lax.psum((dot_rows(every, features), cross), "feat")
        first = lax.dot_general(
            turned,
            by_step(share, steps, per),
            (((2,), (1,)), ((0,), (0,))),
            precision=lax.Precision.HIGHEST,
            preferred_element_type=jnp.float32,
        )
        return [gram, cross], first


def local(features, targets, block_index, inverse):
    rank = lax.axis_index("rows")
    row_count = lax.axis_size("rows")
    rows = features.shape[0]
    steps, block = block_index.shape
    per = block // row_count
    fits = rows == len(pairs_of(steps)) * block and per % 16 == 0 and features.shape[1] % (128 * PIECES) == 0
    lined = fits and (row_count, lax.axis_size("feat")) == (8, 4)
    mover = Lines() if lined else Gathers()

    place = jnp.arange(block)
    moved = jnp.repeat(mover.order, per) * per + place % per
    swap = moved[:, None] == place[None, :]
    picks = jnp.sum(jnp.where(swap[None], block_index[:, None, :], 0), axis=2)
    swap = swap.astype(jnp.float32)
    turned = jnp.stack([exact_dot(exact_dot(swap, inverse[step]), swap.T) for step in range(steps)])
    same = jnp.concatenate(
        [
            (picks[step][:, None] == picks[before][None, :]).astype(jnp.float32)
            for step, before in pairs_of(steps)
        ],
        axis=1,
    )
    own = picks[:, :per].reshape(-1, 1) - rank * rows

    sums, first = mover.run(features, targets, block_index, turned, per)
    operands = sums + [same, first, turned, own, targets]
    out = jax.ShapeDtypeStruct(targets.shape, jnp.float32)
    return pl.pallas_call(
        functools.partial(finish_kernel, steps, per, lined),
        out_shape=(out, out),
        in_specs=([SMEM] if lined else []) + [VMEM] * (len(operands) - lined),
        out_specs=(VMEM, VMEM),
        compiler_params=PARAMS,
        cost_estimate=cost(3 * rows * steps * block, targets.shape[1]),
    )(*operands)


def solution(mesh):
    return jax.shard_map(
        local,
        mesh=mesh,
        in_specs=(P("rows", "feat"), P("rows", None), P(), P()),
        out_specs=(P("rows", None), P("rows", None)),
        check_vma=False,
    )
```

```python
import functools

import jax
import jax.numpy as jnp
from jax import lax
from jax.experimental import pallas as pl
from jax.experimental.pallas import tpu as pltpu
from jax.sharding import PartitionSpec as P

F = 24576
VMEM = pl.BlockSpec(memory_space=pltpu.VMEM)
SMEM = pl.BlockSpec(memory_space=pltpu.SMEM)
HBM = pl.BlockSpec(memory_space=pltpu.HBM)
PIECES = 4
PARAMS = pltpu.CompilerParams(vmem_limit_bytes=24 * 1024 * 1024)
PICK = pltpu.CompilerParams(vmem_limit_bytes=58 * 1024 * 1024)
GRAM = pltpu.CompilerParams(vmem_limit_bytes=46 * 1024 * 1024)


def quadratic(gram):
    scaled = gram * (1.0 / F)
    return scaled + scaled * scaled


def dot_rows(left, right):
    return lax.dot_general(
        left, right, (((1,), (1,)), ((), ())), preferred_element_type=jnp.float32
    )


def exact_dot(left, right):
    return jnp.dot(
        left, right, precision=lax.Precision.HIGHEST, preferred_element_type=jnp.float32
    )


def split(array):
    high = array.astype(jnp.bfloat16)
    return high, (array - high.astype(jnp.float32)).astype(jnp.bfloat16)


def fine_dot(left, right, contract=1):
    sides = (((contract,), (0,)), ((), ()))
    left_high, left_low = left if isinstance(left, tuple) else split(left)
    right_high, right_low = right if isinstance(right, tuple) else split(right)

    def part(one, other):
        return lax.dot_general(one, other, sides, preferred_element_type=jnp.float32)

    return part(left_high, right_high) + (part(left_high, right_low) + part(left_low, right_high))


def pairs_of(steps):
    return [(step, before) for step in range(steps) for before in range(step)]


def of_step(slots, step, per):
    return jnp.concatenate([slot[step * per : (step + 1) * per] for slot in slots], axis=0)


def by_step(array, steps, per):
    parts = array.reshape(-1, steps, per, array.shape[-1])
    return jnp.swapaxes(parts, 0, 1).reshape(steps, -1, array.shape[-1])


def cost(rows, columns):
    return pl.CostEstimate(flops=2 * rows * columns, bytes_accessed=4 * rows, transcendentals=0)


def finish_kernel(steps, per, last, *refs):
    refs = list(refs)
    if last:
        place_ref, early_ref, cross_ref, mine_ref, other_ref = refs[:5]
        refs = refs[5:]
    else:
        gram_ref, cross_ref = refs[:2]
        refs = refs[2:]
    same_ref, first_ref, inverse_ref, own_ref, targets_ref, resid_ref, coeff_ref = refs
    block = first_ref.shape[1]
    rows = targets_ref.shape[0]
    if last:
        core = place_ref[1]
        mine, other = mine_ref[...], other_ref[...]
        end_gram = quadratic(jnp.where(core == 0, mine, other))
        end = jnp.where(core == 0, other, mine)
        count = steps * per
        begun = block - end.shape[0] // steps
        column = lax.broadcasted_iota(jnp.int32, (block, block), 0) < begun

        def end_of(array, step):
            slots = [array[i : i + count] for i in range(0, array.shape[0], count)]
            return of_step(slots, step, per)

        def of(one, other):
            part = end_of(end, one)[:, other * block : (other + 1) * block]
            return jnp.concatenate([jnp.zeros((begun, block), jnp.float32), part], axis=0)

    between = {}
    for at, (step, before) in enumerate(pairs_of(steps)):
        part = cross_ref[:, at * block : (at + 1) * block]
        if last:
            part = part + of(step, before) + jnp.where(column, of(before, step).T, 0.0)
        between[step, before] = split(quadratic(part) + same_ref[:, at * block : (at + 1) * block])
    deltas = []
    for step in range(steps):
        delta = first_ref[step]
        if step:
            change = fine_dot(between[step, 0], deltas[0])
            for before in range(1, step):
                change += fine_dot(between[step, before], deltas[before])
            delta = delta - fine_dot(inverse_ref[step], change)
        deltas.append(split(delta))
    spread = own_ref[...] == lax.broadcasted_iota(jnp.int32, (steps * per, rows), 1)
    spread = spread.astype(jnp.float32).astype(jnp.bfloat16)
    sides = (((0,), (0,)), ((), ()))
    coeffs = jnp.zeros(targets_ref.shape, jnp.float32)
    resid = targets_ref[...]
    for high_or_low in (0, 1):
        own = jnp.concatenate([delta[high_or_low][:per] for delta in deltas], axis=0)
        coeffs += lax.dot_general(spread, own, sides, preferred_element_type=jnp.float32)
    coeff_ref[...] = coeffs
    for step in range(steps):
        if last:
            part = split(end_of(end_gram, step))
            kernel = tuple(
                jnp.concatenate([early_ref[i, step], part[i]], axis=0) for i in range(2)
            )
        else:
            kernel = quadratic(gram_ref[...].reshape(-1, steps, per, rows)[:, step].reshape(block, rows))
        resid = resid - fine_dot(kernel, deltas[step], 0)
    resid_ref[...] = resid - coeffs


def ready_kernel(steps, per, place_ref, *refs):
    mine_ref, other_ref, inverse_ref, *gram_refs, first_ref, early_ref, cross_ref = refs
    core = place_ref[1]
    block = inverse_ref.shape[1]
    half = mine_ref.shape[1]
    for step in range(steps):
        rows = slice(step * block, (step + 1) * block)
        inverse = split(inverse_ref[step])
        mine, other = mine_ref[rows], other_ref[rows]
        first_ref[step, :, :half] = fine_dot(inverse, jnp.where(core == 0, mine, other))
        first_ref[step, :, half:] = fine_dot(inverse, jnp.where(core == 0, other, mine))
    mine, other = gram_refs[0][...], gram_refs[1][...]
    gram = jnp.concatenate([jnp.where(core == 0, mine, other), jnp.where(core == 0, other, mine)], axis=0)
    cross_ref[...] = gram[-block:]
    kernel = quadratic(gram[:-block])
    kernel = kernel.reshape(-1, steps, per, kernel.shape[-1])
    for step in range(steps):
        early_ref[0, step], early_ref[1, step] = split(kernel[:, step].reshape(early_ref.shape[2:]))


def pieces_of(features_ref):
    width = features_ref.shape[1] // PIECES
    return [slice(i * width, (i + 1) * width) for i in range(PIECES)]


def fetch(features_ref, held_ref, sems):
    copies = []
    for i, at in enumerate(pieces_of(features_ref)):
        copies.append(pltpu.make_async_copy(features_ref.at[:, at], held_ref.at[:, at], sems.at[i]))
        copies[-1].start()
    return copies


def held(features):
    return [pltpu.VMEM(features.shape, features.dtype), pltpu.SemaphoreType.DMA((PIECES,))]


def add(total, part):
    return part if total is None else total + part


def pick_kernel(
    per, index_hbm, place_ref, features_ref, targets_ref, out_ref, index_ref, held_targets, side_sems, held_ref, sems
):
    index = pltpu.make_async_copy(index_hbm, index_ref, side_sems.at[0])
    index.start()
    side = pltpu.make_async_copy(targets_ref, held_targets, side_sems.at[1])
    side.start()
    copies = fetch(features_ref, held_ref, sems)
    index.wait()
    rank, core = place_ref[0], place_ref[1]
    rows, columns = features_ref.shape
    steps = index_ref.shape[0]
    line = lax.broadcasted_iota(jnp.int32, (steps * per, rows), 0)
    wanted = jnp.zeros((steps * per, rows), jnp.int32)
    for step in range(steps):
        for i in range(per):
            wanted = jnp.where(line == step * per + i, index_ref[step, rank * per + i], wanted)
    chosen = wanted - rank * rows == lax.broadcasted_iota(jnp.int32, wanted.shape, 1)
    chosen = chosen.astype(jnp.float32).astype(jnp.bfloat16)

    def take(array):
        return jnp.dot(chosen, array, preferred_element_type=jnp.float32).astype(jnp.bfloat16)

    side.wait()
    width = targets_ref.shape[1] // 2
    values = jnp.where(core == 0, held_targets[:, :width], held_targets[:, width:])
    high, low = split(values)
    out_ref[:, columns : columns + width] = take(high)
    out_ref[:, columns + width :] = take(low)
    for copy, at in zip(copies, pieces_of(features_ref)):
        copy.wait()
        out_ref[:, at] = take(held_ref[:, at])


def pick(block_index, place, features, targets, per):
    count = block_index.shape[0] * per
    wide = features.shape[1] + targets.shape[1]
    return pl.pallas_call(
        functools.partial(pick_kernel, per),
        out_shape=jax.ShapeDtypeStruct((count, wide), features.dtype),
        in_specs=[HBM, SMEM, HBM, HBM],
        out_specs=VMEM,
        scratch_shapes=[
            pltpu.SMEM(block_index.shape, jnp.int32),
            pltpu.VMEM(targets.shape, jnp.float32),
            pltpu.SemaphoreType.DMA((2,)),
        ]
        + held(features),
        compiler_params=PICK,
        cost_estimate=cost(count * features.shape[0], wide),
    )(block_index, place, features, targets)


def gram_kernel(steps, per, missing, place_ref, *refs):
    *slot_refs, features_ref, keep_ref, send_ref, held_ref, sems = refs
    copies = fetch(features_ref, held_ref, sems)
    total = [None] * (1 + len(pairs_of(steps)))
    for at in pieces_of(features_ref):
        slots = [ref[:, at] for ref in slot_refs]
        slots += [jnp.zeros_like(slots[0])] * missing
        rows = [of_step(slots, step, per) for step in range(steps)]
        for i, (step, before) in enumerate(pairs_of(steps)):
            total[1 + i] = add(total[1 + i], dot_rows(rows[step], rows[before]))
    for copy, at in zip(copies, pieces_of(features_ref)):
        slots = jnp.concatenate([ref[:, at] for ref in slot_refs], axis=0)
        copy.wait()
        total[0] = add(total[0], dot_rows(slots, held_ref[:, at]))
    total = jnp.concatenate([total[0], jnp.concatenate(total[1:], axis=1)], axis=0)
    half = keep_ref.shape[0]
    core = place_ref[1]
    keep_ref[...] = jnp.where(core == 0, total[:half], total[half:])
    send_ref[...] = jnp.where(core == 0, total[half:], total[:half])


def last_kernel(steps, per, begun, place_ref, *refs):
    *slot_refs, inner_ref, left_ref, right_ref, features_ref = refs[:-5]
    keep_ref, send_ref, first_ref, held_ref, sems = refs[-5:]
    core = place_ref[1]
    inner = place_ref[2] == 1
    columns = features_ref.shape[1]
    copies = fetch(features_ref, held_ref, sems)

    def slots_at(at):
        slots = [ref[:, at] for ref in slot_refs]
        other = slots.pop()
        slots[-1] = jnp.where(inner, slots[-1], other)
        last = jnp.where(core == 0, left_ref[:, at], right_ref[:, at])
        return slots + [jnp.where(inner, inner_ref[:, at], last)]

    def every(slots):
        return jnp.concatenate([of_step(slots, step, per) for step in range(steps)], axis=0)

    total, cross = None, None
    for at in pieces_of(features_ref):
        slots = slots_at(at)
        cross = add(cross, dot_rows(every(slots), jnp.concatenate(slots[begun:], axis=0)))
    for copy, at in zip(copies, pieces_of(features_ref)):
        new = jnp.concatenate(slots_at(at)[begun:], axis=0)
        copy.wait()
        total = add(total, dot_rows(held_ref[:, at], new))
    total, cross = total.T, cross.T
    keep_ref[...] = jnp.where(core == 0, total, cross)
    send_ref[...] = jnp.where(core == 0, cross, total)
    width = (inner_ref.shape[1] - columns) // 2
    high = every(slots_at(slice(columns, columns + width)))
    low = every(slots_at(slice(columns + width, columns + 2 * width)))
    first_ref[...] = high.astype(jnp.float32) + low.astype(jnp.float32)


class Lines:
    def __init__(self):
        self.beside = [(r, r ^ 1) for r in range(8)]
        self.pair = [(r, r ^ 2) for r in range(8)]
        self.inner = [(r, r ^ 6) for r in range(2, 6)]
        self.outer = [(2, 0), (3, 1), (4, 6), (5, 7)]
        ends = [(r, r ^ 1) for r in (0, 1, 6, 7)]
        self.ends = [(4 * r + f, 4 * to + f) for r, to in ends for f in (0, 2)]
        self.outer_second = [(4 * r + f, 4 * to + f) for r, to in self.outer for f in (1, 3)]
        rank = lax.axis_index("rows")
        core = lax.axis_index("feat") % 2
        self.is_inner = (rank >= 2) & (rank < 6)
        self.order = rank ^ jnp.arange(8)
        self.place = jnp.stack([rank, core, self.is_inner.astype(jnp.int32)])

    def near(self, array, bit):
        return lax.ppermute(array, "feat", [(f, f ^ bit) for f in range(4)])

    def send(self, array, pairs):
        return lax.ppermute(array, "rows", pairs)

    def run(self, features, targets, block_index, turned, per):
        rows, columns = features.shape
        steps, block = block_index.shape
        count = steps * per
        hold = lax.optimization_barrier
        own = pick(block_index, self.place, features, targets, per)

        pair = self.send(own, self.pair)
        mid = self.send(own, self.inner)
        own_b = self.send(own, self.beside)
        pair, mid, own_b = hold((pair, mid, own_b))

        far = self.send(pair, self.inner)
        mid_end = self.send(mid, self.outer)
        pair_b = self.send(pair, self.beside)
        far, mid_end, pair_b, own_b = hold((far, mid_end, pair_b, own_b))

        third = jnp.where(self.is_inner, far, mid_end)
        third_b = self.send(third, self.beside)
        far_end = self.send(far, self.outer)
        last_in = self.send(own_b, self.inner)
        slots = [own, own_b, pair, pair_b, third]
        begun = len(slots)
        part = jax.ShapeDtypeStruct(((begun * count + block) // 2, rows), jnp.float32)
        gram, given = pl.pallas_call(
            functools.partial(gram_kernel, steps, per, 8 - begun),
            out_shape=(part, part),
            in_specs=[SMEM] + [VMEM] * begun + [HBM],
            out_specs=(VMEM, VMEM),
            scratch_shapes=held(features),
            compiler_params=GRAM,
            cost_estimate=cost((begun * count + block) * rows, columns),
        )(self.place, *slots, features)
        gram = gram + self.near(given, 1)
        third_b, far_end, last_in, gram = hold((third_b, far_end, last_in, gram))

        left = lax.ppermute(far_end, ("rows", "feat"), self.ends)
        right = lax.ppermute(third_b, ("rows", "feat"), self.outer_second)
        gram_near = self.near(gram, 2)
        left, right, gram_near = hold((left, right, gram_near))
        gram = gram + gram_near

        slots = slots + [third_b, mid, far_end, last_in, left, right]
        end = jax.ShapeDtypeStruct(((8 - begun) * count, rows), jnp.float32)
        keep, given, first = pl.pallas_call(
            functools.partial(last_kernel, steps, per, begun),
            out_shape=(
                end,
                end,
                jax.ShapeDtypeStruct((steps * block, targets.shape[1] // 2), jnp.float32),
            ),
            in_specs=[SMEM] + [VMEM] * len(slots) + [HBM],
            out_specs=(VMEM,) * 3,
            scratch_shapes=held(features),
            compiler_params=GRAM,
            cost_estimate=cost((8 - begun) * count * (rows + steps * block), columns),
        )(self.place, *slots, features)
        keep = keep + self.near(given, 1)
        keep_near = self.near(keep, 2)
        first, early, cross = pl.pallas_call(
            functools.partial(ready_kernel, steps, per),
            out_shape=(
                jax.ShapeDtypeStruct((steps, block, targets.shape[1]), jnp.float32),
                jax.ShapeDtypeStruct((2, steps, begun * per, rows), jnp.bfloat16),
                jax.ShapeDtypeStruct((block, rows), jnp.float32),
            ),
            in_specs=[SMEM] + [VMEM] * 5,
            out_specs=(VMEM,) * 3,
            compiler_params=PARAMS,
            cost_estimate=cost(3 * steps * block * block, targets.shape[1]),
        )(self.place, first, self.near(first, 1), turned, gram, self.near(gram, 1))
        keep, first = hold((keep + keep_near, first))
        return [self.place, early, cross, keep, self.near(keep, 1)], first


class Gathers:
    def __init__(self):
        size = lax.axis_size("rows")
        self.order = (lax.axis_index("rows") + jnp.arange(size)) % size

    def turn(self, own):
        every = lax.all_gather(own, "rows", axis=0, tiled=True)
        start = lax.axis_index("rows") * own.shape[0]
        return lax.dynamic_slice_in_dim(
            jnp.concatenate([every, every], axis=0), start, every.shape[0], 0
        )

    def run(self, features, targets, block_index, turned, per):
        steps = block_index.shape[0]
        rank = lax.axis_index("rows")
        picks = lax.dynamic_slice_in_dim(block_index, rank * per, per, 1).reshape(-1)
        picks = picks - rank * features.shape[0]
        every = self.turn(jnp.take(features, picks, axis=0))
        width = targets.shape[1] // lax.axis_size("feat")
        start = lax.axis_index("feat") * width
        share = jnp.take(lax.dynamic_slice_in_dim(targets, start, width, 1), picks, axis=0)
        share = lax.all_gather(self.turn(share), "feat", axis=1, tiled=True)
        blocks = by_step(every, steps, per)
        cross = jnp.concatenate(
            [dot_rows(blocks[step], blocks[before]) for step, before in pairs_of(steps)], axis=1
        )
        gram, cross = lax.psum((dot_rows(every, features), cross), "feat")
        first = lax.dot_general(
            turned,
            by_step(share, steps, per),
            (((2,), (1,)), ((0,), (0,))),
            precision=lax.Precision.HIGHEST,
            preferred_element_type=jnp.float32,
        )
        return [gram, cross], first


def local(features, targets, block_index, inverse):
    rank = lax.axis_index("rows")
    row_count = lax.axis_size("rows")
    rows = features.shape[0]
    steps, block = block_index.shape
    per = block // row_count
    fits = rows == len(pairs_of(steps)) * block and per % 16 == 0 and features.shape[1] % (128 * PIECES) == 0
    lined = fits and (row_count, lax.axis_size("feat")) == (8, 4)
    mover = Lines() if lined else Gathers()

    place = jnp.arange(block)
    moved = jnp.repeat(mover.order, per) * per + place % per
    swap = moved[:, None] == place[None, :]
    picks = jnp.sum(jnp.where(swap[None], block_index[:, None, :], 0), axis=2)
    swap = swap.astype(jnp.float32)
    turned = jnp.stack([exact_dot(exact_dot(swap, inverse[step]), swap.T) for step in range(steps)])
    same = jnp.concatenate(
        [
            (picks[step][:, None] == picks[before][None, :]).astype(jnp.float32)
            for step, before in pairs_of(steps)
        ],
        axis=1,
    )
    own = picks[:, :per].reshape(-1, 1) - rank * rows

    sums, first = mover.run(features, targets, block_index, turned, per)
    operands = sums + [same, first, turned, own, targets]
    out = jax.ShapeDtypeStruct(targets.shape, jnp.float32)
    return pl.pallas_call(
        functools.partial(finish_kernel, steps, per, lined),
        out_shape=(out, out),
        in_specs=([SMEM] if lined else []) + [VMEM] * (len(operands) - lined),
        out_specs=(VMEM, VMEM),
        compiler_params=PARAMS,
        cost_estimate=cost(3 * rows * steps * block, targets.shape[1]),
    )(*operands)


def solution(mesh):
    return jax.shard_map(
        local,
        mesh=mesh,
        in_specs=(P("rows", "feat"), P("rows", None), P(), P()),
        out_specs=(P("rows", None), P("rows", None)),
        check_vma=False,
    )
```

```python
import functools

import jax
import jax.numpy as jnp
from jax import lax
from jax.experimental import pallas as pl
from jax.experimental.pallas import tpu as pltpu
from jax.sharding import PartitionSpec as P

F = 24576
VMEM = pl.BlockSpec(memory_space=pltpu.VMEM)
SMEM = pl.BlockSpec(memory_space=pltpu.SMEM)
HBM = pl.BlockSpec(memory_space=pltpu.HBM)
PIECES = 4
PARAMS = pltpu.CompilerParams(vmem_limit_bytes=24 * 1024 * 1024)
PICK = pltpu.CompilerParams(vmem_limit_bytes=58 * 1024 * 1024)
GRAM = pltpu.CompilerParams(vmem_limit_bytes=46 * 1024 * 1024)


def quadratic(gram):
    scaled = gram * (1.0 / F)
    return scaled + scaled * scaled


def dot_rows(left, right):
    return lax.dot_general(
        left, right, (((1,), (1,)), ((), ())), preferred_element_type=jnp.float32
    )


def exact_dot(left, right):
    return jnp.dot(
        left, right, precision=lax.Precision.HIGHEST, preferred_element_type=jnp.float32
    )


def split(array):
    high = array.astype(jnp.bfloat16)
    return high, (array - high.astype(jnp.float32)).astype(jnp.bfloat16)


def fine_dot(left, right, contract=1):
    sides = (((contract,), (0,)), ((), ()))
    left_high, left_low = left if isinstance(left, tuple) else split(left)
    right_high, right_low = right if isinstance(right, tuple) else split(right)

    def part(one, other):
        return lax.dot_general(one, other, sides, preferred_element_type=jnp.float32)

    return part(left_high, right_high) + (part(left_high, right_low) + part(left_low, right_high))


def pairs_of(steps):
    return [(step, before) for step in range(steps) for before in range(step)]


def of_step(slots, step, per):
    return jnp.concatenate([slot[step * per : (step + 1) * per] for slot in slots], axis=0)


def by_step(array, steps, per):
    parts = array.reshape(-1, steps, per, array.shape[-1])
    return jnp.swapaxes(parts, 0, 1).reshape(steps, -1, array.shape[-1])


def cost(rows, columns):
    return pl.CostEstimate(flops=2 * rows * columns, bytes_accessed=4 * rows, transcendentals=0)


def finish_kernel(steps, per, last, *refs):
    refs = list(refs)
    if last:
        place_ref, early_ref, cross_ref, mine_ref, other_ref = refs[:5]
        refs = refs[5:]
    else:
        gram_ref, cross_ref = refs[:2]
        refs = refs[2:]
    same_ref, first_ref, inverse_ref, own_ref, targets_ref, resid_ref, coeff_ref = refs
    block = first_ref.shape[1]
    rows = targets_ref.shape[0]
    if last:
        core = place_ref[1]
        mine, other = mine_ref[...], other_ref[...]
        end_gram = quadratic(jnp.where(core == 0, mine, other))
        end = jnp.where(core == 0, other, mine)
        count = steps * per
        begun = block - end.shape[0] // steps
        column = lax.broadcasted_iota(jnp.int32, (block, block), 0) < begun

        def end_of(array, step):
            slots = [array[i : i + count] for i in range(0, array.shape[0], count)]
            return of_step(slots, step, per)

        def of(one, other):
            part = end_of(end, one)[:, other * block : (other + 1) * block]
            return jnp.concatenate([jnp.zeros((begun, block), jnp.float32), part], axis=0)

    between = {}
    for at, (step, before) in enumerate(pairs_of(steps)):
        part = cross_ref[:, at * block : (at + 1) * block]
        if last:
            part = part + of(step, before) + jnp.where(column, of(before, step).T, 0.0)
        between[step, before] = split(quadratic(part) + same_ref[:, at * block : (at + 1) * block])
    deltas = []
    for step in range(steps):
        delta = first_ref[step]
        if step:
            change = fine_dot(between[step, 0], deltas[0])
            for before in range(1, step):
                change += fine_dot(between[step, before], deltas[before])
            delta = delta - fine_dot(inverse_ref[step], change)
        deltas.append(split(delta))
    spread = own_ref[...] == lax.broadcasted_iota(jnp.int32, (steps * per, rows), 1)
    spread = spread.astype(jnp.float32).astype(jnp.bfloat16)
    sides = (((0,), (0,)), ((), ()))
    coeffs = jnp.zeros(targets_ref.shape, jnp.float32)
    resid = targets_ref[...]
    for high_or_low in (0, 1):
        own = jnp.concatenate([delta[high_or_low][:per] for delta in deltas], axis=0)
        coeffs += lax.dot_general(spread, own, sides, preferred_element_type=jnp.float32)
    coeff_ref[...] = coeffs
    for step in range(steps):
        if last:
            part = split(end_of(end_gram, step))
            kernel = tuple(
                jnp.concatenate([early_ref[i, step], part[i]], axis=0) for i in range(2)
            )
        else:
            kernel = quadratic(gram_ref[...].reshape(-1, steps, per, rows)[:, step].reshape(block, rows))
        resid = resid - fine_dot(kernel, deltas[step], 0)
    resid_ref[...] = resid - coeffs


def ready_kernel(steps, per, place_ref, *refs):
    mine_ref, other_ref, inverse_ref, *gram_refs, first_ref, early_ref, cross_ref = refs
    core = place_ref[1]
    block = inverse_ref.shape[1]
    half = mine_ref.shape[1]
    for step in range(steps):
        rows = slice(step * block, (step + 1) * block)
        inverse = split(inverse_ref[step])
        mine, other = mine_ref[rows], other_ref[rows]
        first_ref[step, :, :half] = fine_dot(inverse, jnp.where(core == 0, mine, other))
        first_ref[step, :, half:] = fine_dot(inverse, jnp.where(core == 0, other, mine))
    mine, other = gram_refs[0][...], gram_refs[1][...]
    gram = jnp.concatenate([jnp.where(core == 0, mine, other), jnp.where(core == 0, other, mine)], axis=0)
    cross_ref[...] = gram[-block:]
    kernel = quadratic(gram[:-block])
    kernel = kernel.reshape(-1, steps, per, kernel.shape[-1])
    for step in range(steps):
        early_ref[0, step], early_ref[1, step] = split(kernel[:, step].reshape(early_ref.shape[2:]))


def pieces_of(features_ref):
    width = features_ref.shape[1] // PIECES
    return [slice(i * width, (i + 1) * width) for i in range(PIECES)]


def fetch(features_ref, held_ref, sems):
    copies = []
    for i, at in enumerate(pieces_of(features_ref)):
        copies.append(pltpu.make_async_copy(features_ref.at[:, at], held_ref.at[:, at], sems.at[i]))
        copies[-1].start()
    return copies


def held(features):
    return [pltpu.VMEM(features.shape, features.dtype), pltpu.SemaphoreType.DMA((PIECES,))]


def add(total, part):
    return part if total is None else total + part


def pick_kernel(
    per, index_hbm, place_ref, features_ref, targets_ref, out_ref, index_ref, held_targets, side_sems, held_ref, sems
):
    index = pltpu.make_async_copy(index_hbm, index_ref, side_sems.at[0])
    index.start()
    copies = fetch(features_ref, held_ref, sems)
    side = pltpu.make_async_copy(targets_ref, held_targets, side_sems.at[1])
    side.start()
    index.wait()
    rank, core = place_ref[0], place_ref[1]
    rows, columns = features_ref.shape
    steps = index_ref.shape[0]
    line = lax.broadcasted_iota(jnp.int32, (steps * per, 128), 0)
    wanted = jnp.zeros((steps * per, 128), jnp.int32)
    for step in range(steps):
        for i in range(per):
            wanted = jnp.where(line == step * per + i, index_ref[step, rank * per + i], wanted)
    chosen = wanted[:, :1] - rank * rows == lax.broadcasted_iota(jnp.int32, (steps * per, rows), 1)
    chosen = chosen.astype(jnp.float32).astype(jnp.bfloat16)

    def take(array):
        return jnp.dot(chosen, array, preferred_element_type=jnp.float32).astype(jnp.bfloat16)

    for copy, at in zip(copies, pieces_of(features_ref)):
        copy.wait()
        out_ref[:, at] = take(held_ref[:, at])
    side.wait()
    width = targets_ref.shape[1] // 2
    values = jnp.where(core == 0, held_targets[:, :width], held_targets[:, width:])
    high, low = split(values)
    out_ref[:, columns : columns + width] = take(high)
    out_ref[:, columns + width :] = take(low)


def pick(block_index, place, features, targets, per):
    count = block_index.shape[0] * per
    wide = features.shape[1] + targets.shape[1]
    return pl.pallas_call(
        functools.partial(pick_kernel, per),
        out_shape=jax.ShapeDtypeStruct((count, wide), features.dtype),
        in_specs=[HBM, SMEM, HBM, HBM],
        out_specs=VMEM,
        scratch_shapes=[
            pltpu.SMEM(block_index.shape, jnp.int32),
            pltpu.VMEM(targets.shape, jnp.float32),
            pltpu.SemaphoreType.DMA((2,)),
        ]
        + held(features),
        compiler_params=PICK,
        cost_estimate=cost(count * features.shape[0], wide),
    )(block_index, place, features, targets)


def gram_kernel(steps, per, missing, place_ref, *refs):
    *slot_refs, features_ref, keep_ref, send_ref, held_ref, sems = refs
    copies = fetch(features_ref, held_ref, sems)
    total = [None] * (1 + len(pairs_of(steps)))
    for at in pieces_of(features_ref):
        slots = [ref[:, at] for ref in slot_refs]
        slots += [jnp.zeros_like(slots[0])] * missing
        rows = [of_step(slots, step, per) for step in range(steps)]
        for i, (step, before) in enumerate(pairs_of(steps)):
            total[1 + i] = add(total[1 + i], dot_rows(rows[step], rows[before]))
    for copy, at in zip(copies, pieces_of(features_ref)):
        slots = jnp.concatenate([ref[:, at] for ref in slot_refs], axis=0)
        copy.wait()
        total[0] = add(total[0], dot_rows(slots, held_ref[:, at]))
    total = jnp.concatenate([total[0], jnp.concatenate(total[1:], axis=1)], axis=0)
    half = keep_ref.shape[0]
    core = place_ref[1]
    keep_ref[...] = jnp.where(core == 0, total[:half], total[half:])
    send_ref[...] = jnp.where(core == 0, total[half:], total[:half])


def last_kernel(steps, per, begun, place_ref, *refs):
    *slot_refs, left_in_ref, right_in_ref, left_ref, right_ref, features_ref = refs[:-5]
    keep_ref, send_ref, first_ref, held_ref, sems = refs[-5:]
    core = place_ref[1]
    inner = place_ref[2] == 1
    columns = features_ref.shape[1]
    copies = fetch(features_ref, held_ref, sems)

    def slots_at(at):
        slots = [ref[:, at] for ref in slot_refs]
        other = slots.pop()
        slots[-1] = jnp.where(inner, slots[-1], other)
        last = jnp.where(core == 0, left_ref[:, at], right_ref[:, at])
        last_in = jnp.where(core == 0, left_in_ref[:, at], right_in_ref[:, at])
        return slots + [jnp.where(inner, last_in, last)]

    def every(slots):
        return jnp.concatenate([of_step(slots, step, per) for step in range(steps)], axis=0)

    rows = features_ref.shape[0]
    both = None
    for copy, at in zip(copies, pieces_of(features_ref)):
        slots = slots_at(at)
        new = jnp.concatenate(slots[begun:], axis=0)
        if both is None:
            cross = dot_rows(every(slots), new)
            copy.wait()
            both = jnp.concatenate([dot_rows(held_ref[:, at], new), cross], axis=0)
        else:
            copy.wait()
            both = both + dot_rows(jnp.concatenate([held_ref[:, at], every(slots)], axis=0), new)
    total, cross = both[:rows], both[rows:]
    total, cross = total.T, cross.T
    keep_ref[...] = jnp.where(core == 0, total, cross)
    send_ref[...] = jnp.where(core == 0, cross, total)
    width = (left_ref.shape[1] - columns) // 2
    high = every(slots_at(slice(columns, columns + width)))
    low = every(slots_at(slice(columns + width, columns + 2 * width)))
    first_ref[...] = high.astype(jnp.float32) + low.astype(jnp.float32)


class Lines:
    def __init__(self):
        self.beside = [(r, r ^ 1) for r in range(8)]
        self.pair = [(r, r ^ 2) for r in range(8)]
        self.inner = [(r, r ^ 6) for r in range(2, 6)]
        self.outer = [(2, 0), (3, 1), (4, 6), (5, 7)]
        ends = [(r, r ^ 1) for r in (0, 1, 6, 7)]
        self.ends = [(4 * r + f, 4 * to + f) for r, to in ends for f in (0, 2)]
        inner = [(r, r ^ 1) for r in range(2, 6)]
        self.inner_beside = [(4 * r + f, 4 * to + f) for r, to in inner for f in (0, 2)]
        self.inner_second = [(4 * r + f, 4 * to + f) for r, to in self.inner for f in (1, 3)]
        self.outer_second = [(4 * r + f, 4 * to + f) for r, to in self.outer for f in (1, 3)]
        rank = lax.axis_index("rows")
        core = lax.axis_index("feat") % 2
        self.is_inner = (rank >= 2) & (rank < 6)
        self.order = rank ^ jnp.arange(8)
        self.place = jnp.stack([rank, core, self.is_inner.astype(jnp.int32)])

    def near(self, array, bit):
        return lax.ppermute(array, "feat", [(f, f ^ bit) for f in range(4)])

    def send(self, array, pairs):
        return lax.ppermute(array, "rows", pairs)

    def run(self, features, targets, block_index, turned, per):
        rows, columns = features.shape
        steps, block = block_index.shape
        count = steps * per
        hold = lax.optimization_barrier
        own = pick(block_index, self.place, features, targets, per)

        pair = self.send(own, self.pair)
        mid = self.send(own, self.inner)
        own_b = self.send(own, self.beside)
        pair, mid, own_b = hold((pair, mid, own_b))

        far = self.send(pair, self.inner)
        mid_end = self.send(mid, self.outer)
        pair_b = self.send(pair, self.beside)
        far, mid_end, pair_b, own_b = hold((far, mid_end, pair_b, own_b))

        third = jnp.where(self.is_inner, far, mid_end)
        third_b = self.send(third, self.beside)
        far_end = self.send(far, self.outer)
        slots = [own, own_b, pair, pair_b, third]
        begun = len(slots)
        part = jax.ShapeDtypeStruct(((begun * count + block) // 2, rows), jnp.float32)
        gram, given = pl.pallas_call(
            functools.partial(gram_kernel, steps, per, 8 - begun),
            out_shape=(part, part),
            in_specs=[SMEM] + [VMEM] * begun + [HBM],
            out_specs=(VMEM, VMEM),
            scratch_shapes=held(features),
            compiler_params=GRAM,
            cost_estimate=cost((begun * count + block) * rows, columns),
        )(self.place, *slots, features)
        gram = gram + self.near(given, 1)
        third_b, far_end, gram, own_b, mid = hold((third_b, far_end, gram, own_b, mid))

        left = lax.ppermute(far_end, ("rows", "feat"), self.ends)
        right = lax.ppermute(third_b, ("rows", "feat"), self.outer_second)
        left_in = lax.ppermute(mid, ("rows", "feat"), self.inner_beside)
        right_in = lax.ppermute(own_b, ("rows", "feat"), self.inner_second)
        gram_near = self.near(gram, 2)
        left, right, left_in, right_in = hold((left, right, left_in, right_in))

        slots = [own, own_b, pair, pair_b, third, third_b, mid, far_end, left_in, right_in, left, right]
        end = jax.ShapeDtypeStruct(((8 - begun) * count, rows), jnp.float32)
        keep, given, first = pl.pallas_call(
            functools.partial(last_kernel, steps, per, begun),
            out_shape=(
                end,
                end,
                jax.ShapeDtypeStruct((steps * block, targets.shape[1] // 2), jnp.float32),
            ),
            in_specs=[SMEM] + [VMEM] * len(slots) + [HBM],
            out_specs=(VMEM,) * 3,
            scratch_shapes=held(features),
            compiler_params=GRAM,
            cost_estimate=cost((8 - begun) * count * (rows + steps * block), columns),
        )(self.place, *slots, features)
        keep = keep + self.near(given, 1)
        keep, gram_near = hold((keep, gram_near))
        gram = gram + gram_near
        keep_near = self.near(keep, 2)
        first, early, cross = pl.pallas_call(
            functools.partial(ready_kernel, steps, per),
            out_shape=(
                jax.ShapeDtypeStruct((steps, block, targets.shape[1]), jnp.float32),
                jax.ShapeDtypeStruct((2, steps, begun * per, rows), jnp.bfloat16),
                jax.ShapeDtypeStruct((block, rows), jnp.float32),
            ),
            in_specs=[SMEM] + [VMEM] * 5,
            out_specs=(VMEM,) * 3,
            compiler_params=PARAMS,
            cost_estimate=cost(3 * steps * block * block, targets.shape[1]),
        )(self.place, first, self.near(first, 1), turned, gram, self.near(gram, 1))
        keep, first = hold((keep, first))
        keep = keep + keep_near
        return [self.place, early, cross, keep, self.near(keep, 1)], first


class Gathers:
    def __init__(self):
        size = lax.axis_size("rows")
        self.order = (lax.axis_index("rows") + jnp.arange(size)) % size

    def turn(self, own):
        every = lax.all_gather(own, "rows", axis=0, tiled=True)
        start = lax.axis_index("rows") * own.shape[0]
        return lax.dynamic_slice_in_dim(
            jnp.concatenate([every, every], axis=0), start, every.shape[0], 0
        )

    def run(self, features, targets, block_index, turned, per):
        steps = block_index.shape[0]
        rank = lax.axis_index("rows")
        picks = lax.dynamic_slice_in_dim(block_index, rank * per, per, 1).reshape(-1)
        picks = picks - rank * features.shape[0]
        every = self.turn(jnp.take(features, picks, axis=0))
        width = targets.shape[1] // lax.axis_size("feat")
        start = lax.axis_index("feat") * width
        share = jnp.take(lax.dynamic_slice_in_dim(targets, start, width, 1), picks, axis=0)
        share = lax.all_gather(self.turn(share), "feat", axis=1, tiled=True)
        blocks = by_step(every, steps, per)
        cross = jnp.concatenate(
            [dot_rows(blocks[step], blocks[before]) for step, before in pairs_of(steps)], axis=1
        )
        gram, cross = lax.psum((dot_rows(every, features), cross), "feat")
        first = lax.dot_general(
            turned,
            by_step(share, steps, per),
            (((2,), (1,)), ((0,), (0,))),
            precision=lax.Precision.HIGHEST,
            preferred_element_type=jnp.float32,
        )
        return [gram, cross], first


def local(features, targets, block_index, inverse):
    rank = lax.axis_index("rows")
    row_count = lax.axis_size("rows")
    rows = features.shape[0]
    steps, block = block_index.shape
    per = block // row_count
    fits = rows == len(pairs_of(steps)) * block and per % 16 == 0 and features.shape[1] % (128 * PIECES) == 0
    lined = fits and (row_count, lax.axis_size("feat")) == (8, 4)
    mover = Lines() if lined else Gathers()

    place = jnp.arange(block)
    moved = jnp.repeat(mover.order, per) * per + place % per
    swap = moved[:, None] == place[None, :]
    picks = jnp.sum(jnp.where(swap[None], block_index[:, None, :], 0), axis=2)
    swap = swap.astype(jnp.float32)
    turned = jnp.stack([exact_dot(exact_dot(swap, inverse[step]), swap.T) for step in range(steps)])
    same = jnp.concatenate(
        [
            (picks[step][:, None] == picks[before][None, :]).astype(jnp.float32)
            for step, before in pairs_of(steps)
        ],
        axis=1,
    )
    own = picks[:, :per].reshape(-1, 1) - rank * rows

    sums, first = mover.run(features, targets, block_index, turned, per)
    operands = sums + [same, first, turned, own, targets]
    out = jax.ShapeDtypeStruct(targets.shape, jnp.float32)
    return pl.pallas_call(
        functools.partial(finish_kernel, steps, per, lined),
        out_shape=(out, out),
        in_specs=([SMEM] if lined else []) + [VMEM] * (len(operands) - lined),
        out_specs=(VMEM, VMEM),
        compiler_params=PARAMS,
        cost_estimate=cost(3 * rows * steps * block, targets.shape[1]),
    )(*operands)


def solution(mesh):
    return jax.shard_map(
        local,
        mesh=mesh,
        in_specs=(P("rows", "feat"), P("rows", None), P(), P()),
        out_specs=(P("rows", None), P("rows", None)),
        check_vma=False,
    )
```

```python
import functools

import jax
import jax.numpy as jnp
from jax import lax
from jax.experimental import pallas as pl
from jax.experimental.pallas import tpu as pltpu
from jax.sharding import PartitionSpec as P

F = 24576
VMEM = pl.BlockSpec(memory_space=pltpu.VMEM)
SMEM = pl.BlockSpec(memory_space=pltpu.SMEM)
HBM = pl.BlockSpec(memory_space=pltpu.HBM)
PIECES = 4
PARAMS = pltpu.CompilerParams(vmem_limit_bytes=24 * 1024 * 1024)
PICK = pltpu.CompilerParams(vmem_limit_bytes=58 * 1024 * 1024)
GRAM = pltpu.CompilerParams(vmem_limit_bytes=46 * 1024 * 1024)


def quadratic(gram):
    scaled = gram * (1.0 / F)
    return scaled + scaled * scaled


def dot_rows(left, right):
    return lax.dot_general(
        left, right, (((1,), (1,)), ((), ())), preferred_element_type=jnp.float32
    )


def exact_dot(left, right):
    return jnp.dot(
        left, right, precision=lax.Precision.HIGHEST, preferred_element_type=jnp.float32
    )


def split(array):
    high = array.astype(jnp.bfloat16)
    return high, (array - high.astype(jnp.float32)).astype(jnp.bfloat16)


def fine_dot(left, right, contract=1):
    sides = (((contract,), (0,)), ((), ()))
    left_high, left_low = left if isinstance(left, tuple) else split(left)
    right_high, right_low = right if isinstance(right, tuple) else split(right)

    def part(one, other):
        return lax.dot_general(one, other, sides, preferred_element_type=jnp.float32)

    return part(left_high, right_high) + (part(left_high, right_low) + part(left_low, right_high))


def pairs_of(steps):
    return [(step, before) for step in range(steps) for before in range(step)]


def of_step(slots, step, per):
    return jnp.concatenate([slot[step * per : (step + 1) * per] for slot in slots], axis=0)


def by_step(array, steps, per):
    parts = array.reshape(-1, steps, per, array.shape[-1])
    return jnp.swapaxes(parts, 0, 1).reshape(steps, -1, array.shape[-1])


def cost(rows, columns):
    return pl.CostEstimate(flops=2 * rows * columns, bytes_accessed=4 * rows, transcendentals=0)


def finish_kernel(steps, per, last, *refs):
    refs = list(refs)
    if last:
        place_ref, early_ref, cross_ref, mine_ref, other_ref = refs[:5]
        refs = refs[5:]
    else:
        gram_ref, cross_ref = refs[:2]
        refs = refs[2:]
    same_ref, first_ref, inverse_ref, own_ref, targets_ref, resid_ref, coeff_ref = refs
    block = first_ref.shape[1]
    rows = targets_ref.shape[0]
    if last:
        core = place_ref[1]
        mine, other = mine_ref[...], other_ref[...]
        end_gram = quadratic(jnp.where(core == 0, mine, other))
        end = jnp.where(core == 0, other, mine)
        count = steps * per
        begun = block - end.shape[0] // steps
        column = lax.broadcasted_iota(jnp.int32, (block, block), 0) < begun

        def end_of(array, step):
            slots = [array[i : i + count] for i in range(0, array.shape[0], count)]
            return of_step(slots, step, per)

        def of(one, other):
            part = end_of(end, one)[:, other * block : (other + 1) * block]
            return jnp.concatenate([jnp.zeros((begun, block), jnp.float32), part], axis=0)

    between = {}
    for at, (step, before) in enumerate(pairs_of(steps)):
        part = cross_ref[:, at * block : (at + 1) * block]
        if last:
            part = part + of(step, before) + jnp.where(column, of(before, step).T, 0.0)
        between[step, before] = split(quadratic(part) + same_ref[:, at * block : (at + 1) * block])
    deltas = []
    for step in range(steps):
        delta = first_ref[step]
        if step:
            change = fine_dot(between[step, 0], deltas[0])
            for before in range(1, step):
                change += fine_dot(between[step, before], deltas[before])
            delta = delta - fine_dot(inverse_ref[step], change)
        deltas.append(split(delta))
    spread = own_ref[...] == lax.broadcasted_iota(jnp.int32, (steps * per, rows), 1)
    spread = spread.astype(jnp.float32).astype(jnp.bfloat16)
    sides = (((0,), (0,)), ((), ()))
    coeffs = jnp.zeros(targets_ref.shape, jnp.float32)
    resid = targets_ref[...]
    for high_or_low in (0, 1):
        own = jnp.concatenate([delta[high_or_low][:per] for delta in deltas], axis=0)
        coeffs += lax.dot_general(spread, own, sides, preferred_element_type=jnp.float32)
    coeff_ref[...] = coeffs
    for step in range(steps):
        if last:
            part = split(end_of(end_gram, step))
            kernel = tuple(
                jnp.concatenate([early_ref[i, step], part[i]], axis=0) for i in range(2)
            )
        else:
            kernel = quadratic(gram_ref[...].reshape(-1, steps, per, rows)[:, step].reshape(block, rows))
        resid = resid - fine_dot(kernel, deltas[step], 0)
    resid_ref[...] = resid - coeffs


def ready_kernel(steps, per, place_ref, *refs):
    mine_ref, other_ref, inverse_ref, *gram_refs, first_ref, early_ref, cross_ref = refs
    core = place_ref[1]
    block = inverse_ref.shape[1]
    half = mine_ref.shape[1]
    for step in range(steps):
        rows = slice(step * block, (step + 1) * block)
        inverse = split(inverse_ref[step])
        mine, other = mine_ref[rows], other_ref[rows]
        first_ref[step, :, :half] = fine_dot(inverse, jnp.where(core == 0, mine, other))
        first_ref[step, :, half:] = fine_dot(inverse, jnp.where(core == 0, other, mine))
    mine, other = gram_refs[0][...], gram_refs[1][...]
    gram = jnp.concatenate([jnp.where(core == 0, mine, other), jnp.where(core == 0, other, mine)], axis=0)
    cross_ref[...] = gram[-block:]
    kernel = quadratic(gram[:-block])
    kernel = kernel.reshape(-1, steps, per, kernel.shape[-1])
    for step in range(steps):
        early_ref[0, step], early_ref[1, step] = split(kernel[:, step].reshape(early_ref.shape[2:]))


def pieces_of(features_ref):
    width = features_ref.shape[1] // PIECES
    return [slice(i * width, (i + 1) * width) for i in range(PIECES)]


def fetch(features_ref, held_ref, sems):
    copies = []
    for i, at in enumerate(pieces_of(features_ref)):
        copies.append(pltpu.make_async_copy(features_ref.at[:, at], held_ref.at[:, at], sems.at[i]))
        copies[-1].start()
    return copies


def held(features):
    return [pltpu.VMEM(features.shape, features.dtype), pltpu.SemaphoreType.DMA((PIECES,))]


def add(total, part):
    return part if total is None else total + part


def pick_kernel(
    per, index_hbm, place_ref, features_ref, targets_ref, out_ref, index_ref, held_targets, side_sems, held_ref, sems
):
    index = pltpu.make_async_copy(index_hbm, index_ref, side_sems.at[0])
    index.start()
    copies = fetch(features_ref, held_ref, sems)
    side = pltpu.make_async_copy(targets_ref, held_targets, side_sems.at[1])
    side.start()
    index.wait()
    rank, core = place_ref[0], place_ref[1]
    rows, columns = features_ref.shape
    steps = index_ref.shape[0]
    line = lax.broadcasted_iota(jnp.int32, (steps * per, 128), 0)
    wanted = jnp.zeros((steps * per, 128), jnp.int32)
    for step in range(steps):
        for i in range(per):
            wanted = jnp.where(line == step * per + i, index_ref[step, rank * per + i], wanted)
    chosen = wanted[:, :1] - rank * rows == lax.broadcasted_iota(jnp.int32, (steps * per, rows), 1)
    chosen = chosen.astype(jnp.float32).astype(jnp.bfloat16)

    def take(array):
        return jnp.dot(chosen, array, preferred_element_type=jnp.float32).astype(jnp.bfloat16)

    for copy, at in zip(copies, pieces_of(features_ref)):
        copy.wait()
        out_ref[:, at] = take(held_ref[:, at])
    side.wait()
    width = targets_ref.shape[1] // 2
    values = jnp.where(core == 0, held_targets[:, :width], held_targets[:, width:])
    high, low = split(values)
    out_ref[:, columns : columns + width] = take(high)
    out_ref[:, columns + width :] = take(low)


def pick(block_index, place, features, targets, per):
    count = block_index.shape[0] * per
    wide = features.shape[1] + targets.shape[1]
    return pl.pallas_call(
        functools.partial(pick_kernel, per),
        out_shape=jax.ShapeDtypeStruct((count, wide), features.dtype),
        in_specs=[HBM, SMEM, HBM, HBM],
        out_specs=VMEM,
        scratch_shapes=[
            pltpu.SMEM(block_index.shape, jnp.int32),
            pltpu.VMEM(targets.shape, jnp.float32),
            pltpu.SemaphoreType.DMA((2,)),
        ]
        + held(features),
        compiler_params=PICK,
        cost_estimate=cost(count * features.shape[0], wide),
    )(block_index, place, features, targets)


def gram_kernel(steps, per, missing, place_ref, *refs):
    *slot_refs, features_ref, keep_ref, send_ref, held_ref, sems = refs
    copies = fetch(features_ref, held_ref, sems)
    total = [None] * (1 + len(pairs_of(steps)))
    for at in pieces_of(features_ref):
        slots = [ref[:, at] for ref in slot_refs]
        slots += [jnp.zeros_like(slots[0])] * missing
        rows = [of_step(slots, step, per) for step in range(steps)]
        for i, (step, before) in enumerate(pairs_of(steps)):
            total[1 + i] = add(total[1 + i], dot_rows(rows[step], rows[before]))
    for copy, at in zip(copies, pieces_of(features_ref)):
        slots = jnp.concatenate([ref[:, at] for ref in slot_refs], axis=0)
        copy.wait()
        total[0] = add(total[0], dot_rows(slots, held_ref[:, at]))
    total = jnp.concatenate([total[0], jnp.concatenate(total[1:], axis=1)], axis=0)
    half = keep_ref.shape[0]
    core = place_ref[1]
    keep_ref[...] = jnp.where(core == 0, total[:half], total[half:])
    send_ref[...] = jnp.where(core == 0, total[half:], total[:half])


def last_kernel(steps, per, begun, place_ref, *refs):
    *slot_refs, inner_ref, left_ref, right_ref, features_ref = refs[:-5]
    keep_ref, send_ref, first_ref, held_ref, sems = refs[-5:]
    core = place_ref[1]
    inner = place_ref[2] == 1
    columns = features_ref.shape[1]
    copies = fetch(features_ref, held_ref, sems)

    def slots_at(at):
        slots = [ref[:, at] for ref in slot_refs]
        other = slots.pop()
        slots[-1] = jnp.where(inner, slots[-1], other)
        last = jnp.where(core == 0, left_ref[:, at], right_ref[:, at])
        return slots + [jnp.where(inner, inner_ref[:, at], last)]

    def every(slots):
        return jnp.concatenate([of_step(slots, step, per) for step in range(steps)], axis=0)

    total, cross = None, None
    for at in pieces_of(features_ref):
        slots = slots_at(at)
        cross = add(cross, dot_rows(every(slots), jnp.concatenate(slots[begun:], axis=0)))
    for copy, at in zip(copies, pieces_of(features_ref)):
        new = jnp.concatenate(slots_at(at)[begun:], axis=0)
        copy.wait()
        total = add(total, dot_rows(held_ref[:, at], new))
    total, cross = total.T, cross.T
    keep_ref[...] = jnp.where(core == 0, total, cross)
    send_ref[...] = jnp.where(core == 0, cross, total)
    width = (inner_ref.shape[1] - columns) // 2
    high = every(slots_at(slice(columns, columns + width)))
    low = every(slots_at(slice(columns + width, columns + 2 * width)))
    first_ref[...] = high.astype(jnp.float32) + low.astype(jnp.float32)


class Lines:
    def __init__(self):
        self.beside = [(r, r ^ 1) for r in range(8)]
        self.pair = [(r, r ^ 2) for r in range(8)]
        self.inner = [(r, r ^ 6) for r in range(2, 6)]
        self.outer = [(2, 0), (3, 1), (4, 6), (5, 7)]
        ends = [(r, r ^ 1) for r in (0, 1, 6, 7)]
        self.ends = [(4 * r + f, 4 * to + f) for r, to in ends for f in (0, 2)]
        self.outer_second = [(4 * r + f, 4 * to + f) for r, to in self.outer for f in (1, 3)]
        rank = lax.axis_index("rows")
        core = lax.axis_index("feat") % 2
        self.is_inner = (rank >= 2) & (rank < 6)
        self.order = rank ^ jnp.arange(8)
        self.place = jnp.stack([rank, core, self.is_inner.astype(jnp.int32)])

    def near(self, array, bit):
        return lax.ppermute(array, "feat", [(f, f ^ bit) for f in range(4)])

    def send(self, array, pairs):
        return lax.ppermute(array, "rows", pairs)

    def run(self, features, targets, block_index, turned, per):
        rows, columns = features.shape
        steps, block = block_index.shape
        count = steps * per
        hold = lax.optimization_barrier
        own = pick(block_index, self.place, features, targets, per)

        pair = self.send(own, self.pair)
        mid = self.send(own, self.inner)
        own_b = self.send(own, self.beside)
        pair, own_b = hold((pair, own_b))

        far = self.send(pair, self.inner)
        mid_end = self.send(mid, self.outer)
        pair_b = self.send(pair, self.beside)
        far, pair_b, own_b = hold((far, pair_b, own_b))

        far_end = self.send(far, self.outer)
        third = jnp.where(self.is_inner, far, mid_end)
        third_b = self.send(third, self.beside)
        last_in = self.send(own_b, self.inner)
        slots = [own, own_b, pair, pair_b, third]
        begun = len(slots)
        part = jax.ShapeDtypeStruct(((begun * count + block) // 2, rows), jnp.float32)
        gram, given = pl.pallas_call(
            functools.partial(gram_kernel, steps, per, 8 - begun),
            out_shape=(part, part),
            in_specs=[SMEM] + [VMEM] * begun + [HBM],
            out_specs=(VMEM, VMEM),
            scratch_shapes=held(features),
            compiler_params=GRAM,
            cost_estimate=cost((begun * count + block) * rows, columns),
        )(self.place, *slots, features)
        gram = gram + self.near(given, 1)
        third_b, far_end, last_in, gram = hold((third_b, far_end, last_in, gram))

        left = lax.ppermute(far_end, ("rows", "feat"), self.ends)
        right = lax.ppermute(third_b, ("rows", "feat"), self.outer_second)
        gram_near = self.near(gram, 2)
        left, right, gram_near = hold((left, right, gram_near))
        gram = gram + gram_near

        slots = slots + [third_b, mid, far_end, last_in, left, right]
        end = jax.ShapeDtypeStruct(((8 - begun) * count, rows), jnp.float32)
        keep, given, first = pl.pallas_call(
            functools.partial(last_kernel, steps, per, begun),
            out_shape=(
                end,
                end,
                jax.ShapeDtypeStruct((steps * block, targets.shape[1] // 2), jnp.float32),
            ),
            in_specs=[SMEM] + [VMEM] * len(slots) + [HBM],
            out_specs=(VMEM,) * 3,
            scratch_shapes=held(features),
            compiler_params=GRAM,
            cost_estimate=cost((8 - begun) * count * (rows + steps * block), columns),
        )(self.place, *slots, features)
        keep = keep + self.near(given, 1)
        keep_near = self.near(keep, 2)
        first, early, cross = pl.pallas_call(
            functools.partial(ready_kernel, steps, per),
            out_shape=(
                jax.ShapeDtypeStruct((steps, block, targets.shape[1]), jnp.float32),
                jax.ShapeDtypeStruct((2, steps, begun * per, rows), jnp.bfloat16),
                jax.ShapeDtypeStruct((block, rows), jnp.float32),
            ),
            in_specs=[SMEM] + [VMEM] * 5,
            out_specs=(VMEM,) * 3,
            compiler_params=PARAMS,
            cost_estimate=cost(3 * steps * block * block, targets.shape[1]),
        )(self.place, first, self.near(first, 1), turned, gram, self.near(gram, 1))
        keep, first = hold((keep + keep_near, first))
        return [self.place, early, cross, keep, self.near(keep, 1)], first


class Gathers:
    def __init__(self):
        size = lax.axis_size("rows")
        self.order = (lax.axis_index("rows") + jnp.arange(size)) % size

    def turn(self, own):
        every = lax.all_gather(own, "rows", axis=0, tiled=True)
        start = lax.axis_index("rows") * own.shape[0]
        return lax.dynamic_slice_in_dim(
            jnp.concatenate([every, every], axis=0), start, every.shape[0], 0
        )

    def run(self, features, targets, block_index, turned, per):
        steps = block_index.shape[0]
        rank = lax.axis_index("rows")
        picks = lax.dynamic_slice_in_dim(block_index, rank * per, per, 1).reshape(-1)
        picks = picks - rank * features.shape[0]
        every = self.turn(jnp.take(features, picks, axis=0))
        width = targets.shape[1] // lax.axis_size("feat")
        start = lax.axis_index("feat") * width
        share = jnp.take(lax.dynamic_slice_in_dim(targets, start, width, 1), picks, axis=0)
        share = lax.all_gather(self.turn(share), "feat", axis=1, tiled=True)
        blocks = by_step(every, steps, per)
        cross = jnp.concatenate(
            [dot_rows(blocks[step], blocks[before]) for step, before in pairs_of(steps)], axis=1
        )
        gram, cross = lax.psum((dot_rows(every, features), cross), "feat")
        first = lax.dot_general(
            turned,
            by_step(share, steps, per),
            (((2,), (1,)), ((0,), (0,))),
            precision=lax.Precision.HIGHEST,
            preferred_element_type=jnp.float32,
        )
        return [gram, cross], first


def local(features, targets, block_index, inverse):
    rank = lax.axis_index("rows")
    row_count = lax.axis_size("rows")
    rows = features.shape[0]
    steps, block = block_index.shape
    per = block // row_count
    fits = rows == len(pairs_of(steps)) * block and per % 16 == 0 and features.shape[1] % (128 * PIECES) == 0
    lined = fits and (row_count, lax.axis_size("feat")) == (8, 4)
    mover = Lines() if lined else Gathers()

    place = jnp.arange(block)
    moved = jnp.repeat(mover.order, per) * per + place % per
    swap = moved[:, None] == place[None, :]
    picks = jnp.sum(jnp.where(swap[None], block_index[:, None, :], 0), axis=2)
    swap = swap.astype(jnp.float32)
    turned = jnp.stack([exact_dot(exact_dot(swap, inverse[step]), swap.T) for step in range(steps)])
    same = jnp.concatenate(
        [
            (picks[step][:, None] == picks[before][None, :]).astype(jnp.float32)
            for step, before in pairs_of(steps)
        ],
        axis=1,
    )
    own = picks[:, :per].reshape(-1, 1) - rank * rows

    sums, first = mover.run(features, targets, block_index, turned, per)
    operands = sums + [same, first, turned, own, targets]
    out = jax.ShapeDtypeStruct(targets.shape, jnp.float32)
    return pl.pallas_call(
        functools.partial(finish_kernel, steps, per, lined),
        out_shape=(out, out),
        in_specs=([SMEM] if lined else []) + [VMEM] * (len(operands) - lined),
        out_specs=(VMEM, VMEM),
        compiler_params=PARAMS,
        cost_estimate=cost(3 * rows * steps * block, targets.shape[1]),
    )(*operands)


def solution(mesh):
    return jax.shard_map(
        local,
        mesh=mesh,
        in_specs=(P("rows", "feat"), P("rows", None), P(), P()),
        out_specs=(P("rows", None), P("rows", None)),
        check_vma=False,
    )
```

```python
import functools

import jax
import jax.numpy as jnp
from jax import lax
from jax.experimental import pallas as pl
from jax.experimental.pallas import tpu as pltpu
from jax.sharding import PartitionSpec as P

F = 24576
VMEM = pl.BlockSpec(memory_space=pltpu.VMEM)
SMEM = pl.BlockSpec(memory_space=pltpu.SMEM)
HBM = pl.BlockSpec(memory_space=pltpu.HBM)
PIECES = 4
PARAMS = pltpu.CompilerParams(vmem_limit_bytes=24 * 1024 * 1024)
PICK = pltpu.CompilerParams(vmem_limit_bytes=58 * 1024 * 1024)
GRAM = pltpu.CompilerParams(vmem_limit_bytes=32 * 1024 * 1024)


def quadratic(gram):
    scaled = gram * (1.0 / F)
    return scaled + scaled * scaled


def dot_rows(left, right):
    return lax.dot_general(
        left, right, (((1,), (1,)), ((), ())), preferred_element_type=jnp.float32
    )


def exact_dot(left, right):
    return jnp.dot(
        left, right, precision=lax.Precision.HIGHEST, preferred_element_type=jnp.float32
    )


def split(array):
    high = array.astype(jnp.bfloat16)
    return high, (array - high.astype(jnp.float32)).astype(jnp.bfloat16)


def fine_dot(left, right, contract=1):
    sides = (((contract,), (0,)), ((), ()))
    left_high, left_low = left if isinstance(left, tuple) else split(left)
    right_high, right_low = right if isinstance(right, tuple) else split(right)

    def part(one, other):
        return lax.dot_general(one, other, sides, preferred_element_type=jnp.float32)

    return part(left_high, right_high) + (part(left_high, right_low) + part(left_low, right_high))


def pairs_of(steps):
    return [(step, before) for step in range(steps) for before in range(step)]


def of_step(slots, step, per):
    return jnp.concatenate([slot[step * per : (step + 1) * per] for slot in slots], axis=0)


def by_step(array, steps, per):
    parts = array.reshape(-1, steps, per, array.shape[-1])
    return jnp.swapaxes(parts, 0, 1).reshape(steps, -1, array.shape[-1])


def cost(rows, columns):
    return pl.CostEstimate(flops=2 * rows * columns, bytes_accessed=4 * rows, transcendentals=0)


def finish_kernel(steps, per, last, *refs):
    refs = list(refs)
    if last:
        place_ref, early_ref, cross_ref, mine_ref, other_ref = refs[:5]
        refs = refs[5:]
    else:
        gram_ref, cross_ref = refs[:2]
        refs = refs[2:]
    same_ref, first_ref, inverse_ref, own_ref, targets_ref, resid_ref, coeff_ref = refs
    block = first_ref.shape[1]
    rows = targets_ref.shape[0]
    if last:
        core = place_ref[1]
        mine, other = mine_ref[...], other_ref[...]
        end_gram = quadratic(jnp.where(core == 0, mine, other))
        end = jnp.where(core == 0, other, mine)
        count = steps * per
        begun = block - end.shape[0] // steps
        column = lax.broadcasted_iota(jnp.int32, (block, block), 0) < begun

        def end_of(array, step):
            slots = [array[i : i + count] for i in range(0, array.shape[0], count)]
            return of_step(slots, step, per)

        def of(one, other):
            part = end_of(end, one)[:, other * block : (other + 1) * block]
            return jnp.concatenate([jnp.zeros((begun, block), jnp.float32), part], axis=0)

    between = {}
    for at, (step, before) in enumerate(pairs_of(steps)):
        part = cross_ref[:, at * block : (at + 1) * block]
        if last:
            part = part + of(step, before) + jnp.where(column, of(before, step).T, 0.0)
        between[step, before] = split(quadratic(part) + same_ref[:, at * block : (at + 1) * block])
    deltas = []
    for step in range(steps):
        delta = first_ref[step]
        if step:
            change = fine_dot(between[step, 0], deltas[0])
            for before in range(1, step):
                change += fine_dot(between[step, before], deltas[before])
            delta = delta - fine_dot(inverse_ref[step], change)
        deltas.append(split(delta))
    spread = own_ref[...] == lax.broadcasted_iota(jnp.int32, (steps * per, rows), 1)
    spread = spread.astype(jnp.float32).astype(jnp.bfloat16)
    sides = (((0,), (0,)), ((), ()))
    coeffs = jnp.zeros(targets_ref.shape, jnp.float32)
    resid = targets_ref[...]
    for high_or_low in (0, 1):
        own = jnp.concatenate([delta[high_or_low][:per] for delta in deltas], axis=0)
        coeffs += lax.dot_general(spread, own, sides, preferred_element_type=jnp.float32)
    coeff_ref[...] = coeffs
    for step in range(steps):
        if last:
            part = split(end_of(end_gram, step))
            kernel = tuple(
                jnp.concatenate([early_ref[i, step], part[i]], axis=0) for i in range(2)
            )
        else:
            kernel = quadratic(gram_ref[...].reshape(-1, steps, per, rows)[:, step].reshape(block, rows))
        resid = resid - fine_dot(kernel, deltas[step], 0)
    resid_ref[...] = resid - coeffs


def ready_kernel(steps, per, place_ref, *refs):
    mine_ref, other_ref, inverse_ref, *gram_refs, first_ref, early_ref, cross_ref = refs
    core = place_ref[1]
    block = inverse_ref.shape[1]
    half = mine_ref.shape[1]
    for step in range(steps):
        rows = slice(step * block, (step + 1) * block)
        inverse = split(inverse_ref[step])
        mine, other = mine_ref[rows], other_ref[rows]
        first_ref[step, :, :half] = fine_dot(inverse, jnp.where(core == 0, mine, other))
        first_ref[step, :, half:] = fine_dot(inverse, jnp.where(core == 0, other, mine))
    mine, other = gram_refs[0][...], gram_refs[1][...]
    gram = jnp.concatenate([jnp.where(core == 0, mine, other), jnp.where(core == 0, other, mine)], axis=0)
    cross_ref[...] = gram[-block:]
    kernel = quadratic(gram[:-block])
    kernel = kernel.reshape(-1, steps, per, kernel.shape[-1])
    for step in range(steps):
        early_ref[0, step], early_ref[1, step] = split(kernel[:, step].reshape(early_ref.shape[2:]))


def pieces_of(features_ref):
    width = features_ref.shape[1] // PIECES
    return [slice(i * width, (i + 1) * width) for i in range(PIECES)]


def fetch(features_ref, held_ref, sems):
    copies = []
    for i, at in enumerate(pieces_of(features_ref)):
        copies.append(pltpu.make_async_copy(features_ref.at[:, at], held_ref.at[:, at], sems.at[i]))
        copies[-1].start()
    return copies


def held(features):
    return [pltpu.VMEM(features.shape, features.dtype), pltpu.SemaphoreType.DMA((PIECES,))]


def add(total, part):
    return part if total is None else total + part


def pick_kernel(
    per, index_hbm, place_ref, features_ref, targets_ref, out_ref, index_ref, held_targets, side_sems, held_ref, sems
):
    index = pltpu.make_async_copy(index_hbm, index_ref, side_sems.at[0])
    index.start()
    copies = fetch(features_ref, held_ref, sems)
    side = pltpu.make_async_copy(targets_ref, held_targets, side_sems.at[1])
    side.start()
    index.wait()
    rank, core = place_ref[0], place_ref[1]
    rows, columns = features_ref.shape
    steps = index_ref.shape[0]
    line = lax.broadcasted_iota(jnp.int32, (steps * per, 128), 0)
    wanted = jnp.zeros((steps * per, 128), jnp.int32)
    for step in range(steps):
        for i in range(per):
            wanted = jnp.where(line == step * per + i, index_ref[step, rank * per + i], wanted)
    chosen = wanted[:, :1] - rank * rows == lax.broadcasted_iota(jnp.int32, (steps * per, rows), 1)
    chosen = chosen.astype(jnp.float32).astype(jnp.bfloat16)

    def take(array):
        return jnp.dot(chosen, array, preferred_element_type=jnp.float32).astype(jnp.bfloat16)

    for copy, at in zip(copies, pieces_of(features_ref)):
        copy.wait()
        out_ref[:, at] = take(held_ref[:, at])
    side.wait()
    width = targets_ref.shape[1] // 2
    values = jnp.where(core == 0, held_targets[:, :width], held_targets[:, width:])
    high, low = split(values)
    out_ref[:, columns : columns + width] = take(high)
    out_ref[:, columns + width :] = take(low)


def pick(block_index, place, features, targets, per):
    count = block_index.shape[0] * per
    wide = features.shape[1] + targets.shape[1]
    return pl.pallas_call(
        functools.partial(pick_kernel, per),
        out_shape=jax.ShapeDtypeStruct((count, wide), features.dtype),
        in_specs=[HBM, SMEM, HBM, HBM],
        out_specs=VMEM,
        scratch_shapes=[
            pltpu.SMEM(block_index.shape, jnp.int32),
            pltpu.VMEM(targets.shape, jnp.float32),
            pltpu.SemaphoreType.DMA((2,)),
        ]
        + held(features),
        compiler_params=PICK,
        cost_estimate=cost(count * features.shape[0], wide),
    )(block_index, place, features, targets)


def gram_kernel(steps, per, missing, place_ref, *refs):
    *slot_refs, features_ref, keep_ref, send_ref = refs
    total = [None] * (1 + len(pairs_of(steps)))
    for at in pieces_of(features_ref):
        slots = [ref[:, at] for ref in slot_refs]
        slots += [jnp.zeros_like(slots[0])] * missing
        rows = [of_step(slots, step, per) for step in range(steps)]
        for i, (step, before) in enumerate(pairs_of(steps)):
            total[1 + i] = add(total[1 + i], dot_rows(rows[step], rows[before]))
    for at in pieces_of(features_ref):
        slots = jnp.concatenate([ref[:, at] for ref in slot_refs], axis=0)
        total[0] = add(total[0], dot_rows(slots, features_ref[:, at]))
    total = jnp.concatenate([total[0], jnp.concatenate(total[1:], axis=1)], axis=0)
    half = keep_ref.shape[0]
    core = place_ref[1]
    keep_ref[...] = jnp.where(core == 0, total[:half], total[half:])
    send_ref[...] = jnp.where(core == 0, total[half:], total[:half])


def last_kernel(steps, per, begun, place_ref, *refs):
    *slot_refs, inner_ref, left_ref, right_ref, features_ref = refs[:-3]
    keep_ref, send_ref, first_ref = refs[-3:]
    core = place_ref[1]
    inner = place_ref[2] == 1
    columns = features_ref.shape[1]

    def slots_at(at):
        slots = [ref[:, at] for ref in slot_refs]
        other = slots.pop()
        slots[-1] = jnp.where(inner, slots[-1], other)
        last = jnp.where(core == 0, left_ref[:, at], right_ref[:, at])
        return slots + [jnp.where(inner, inner_ref[:, at], last)]

    def every(slots):
        return jnp.concatenate([of_step(slots, step, per) for step in range(steps)], axis=0)

    total, cross = None, None
    for at in pieces_of(features_ref):
        slots = slots_at(at)
        cross = add(cross, dot_rows(every(slots), jnp.concatenate(slots[begun:], axis=0)))
    for at in pieces_of(features_ref):
        new = jnp.concatenate(slots_at(at)[begun:], axis=0)
        total = add(total, dot_rows(features_ref[:, at], new))
    total, cross = total.T, cross.T
    keep_ref[...] = jnp.where(core == 0, total, cross)
    send_ref[...] = jnp.where(core == 0, cross, total)
    width = (inner_ref.shape[1] - columns) // 2
    high = every(slots_at(slice(columns, columns + width)))
    low = every(slots_at(slice(columns + width, columns + 2 * width)))
    first_ref[...] = high.astype(jnp.float32) + low.astype(jnp.float32)


class Lines:
    def __init__(self):
        self.beside = [(r, r ^ 1) for r in range(8)]
        self.pair = [(r, r ^ 2) for r in range(8)]
        self.inner = [(r, r ^ 6) for r in range(2, 6)]
        self.outer = [(2, 0), (3, 1), (4, 6), (5, 7)]
        ends = [(r, r ^ 1) for r in (0, 1, 6, 7)]
        self.ends = [(4 * r + f, 4 * to + f) for r, to in ends for f in (0, 2)]
        self.outer_second = [(4 * r + f, 4 * to + f) for r, to in self.outer for f in (1, 3)]
        rank = lax.axis_index("rows")
        core = lax.axis_index("feat") % 2
        self.is_inner = (rank >= 2) & (rank < 6)
        self.order = rank ^ jnp.arange(8)
        self.place = jnp.stack([rank, core, self.is_inner.astype(jnp.int32)])

    def near(self, array, bit):
        return lax.ppermute(array, "feat", [(f, f ^ bit) for f in range(4)])

    def send(self, array, pairs):
        return lax.ppermute(array, "rows", pairs)

    def run(self, features, targets, block_index, turned, per):
        rows, columns = features.shape
        steps, block = block_index.shape
        count = steps * per
        hold = lax.optimization_barrier
        own = pick(block_index, self.place, features, targets, per)

        pair = self.send(own, self.pair)
        mid = self.send(own, self.inner)
        own_b = self.send(own, self.beside)
        pair, own_b = hold((pair, own_b))

        far = self.send(pair, self.inner)
        mid_end = self.send(mid, self.outer)
        pair_b = self.send(pair, self.beside)
        far, pair_b, own_b = hold((far, pair_b, own_b))

        far_end = self.send(far, self.outer)
        third = jnp.where(self.is_inner, far, mid_end)
        third_b = self.send(third, self.beside)
        last_in = self.send(own_b, self.inner)
        slots = [own, own_b, pair, pair_b, third]
        begun = len(slots)
        part = jax.ShapeDtypeStruct(((begun * count + block) // 2, rows), jnp.float32)
        gram, given = pl.pallas_call(
            functools.partial(gram_kernel, steps, per, 8 - begun),
            out_shape=(part, part),
            in_specs=[SMEM] + [VMEM] * begun + [VMEM],
            out_specs=(VMEM, VMEM),
            compiler_params=GRAM,
            cost_estimate=cost((begun * count + block) * rows, columns),
        )(self.place, *slots, features)
        gram = gram + self.near(given, 1)
        third_b, far_end, last_in, gram = hold((third_b, far_end, last_in, gram))

        left = lax.ppermute(far_end, ("rows", "feat"), self.ends)
        right = lax.ppermute(third_b, ("rows", "feat"), self.outer_second)
        gram_near = self.near(gram, 2)
        left, right, gram_near = hold((left, right, gram_near))
        gram = gram + gram_near

        slots = slots + [third_b, mid, far_end, last_in, left, right]
        end = jax.ShapeDtypeStruct(((8 - begun) * count, rows), jnp.float32)
        keep, given, first = pl.pallas_call(
            functools.partial(last_kernel, steps, per, begun),
            out_shape=(
                end,
                end,
                jax.ShapeDtypeStruct((steps * block, targets.shape[1] // 2), jnp.float32),
            ),
            in_specs=[SMEM] + [VMEM] * len(slots) + [VMEM],
            out_specs=(VMEM,) * 3,
            compiler_params=GRAM,
            cost_estimate=cost((8 - begun) * count * (rows + steps * block), columns),
        )(self.place, *slots, features)
        keep = keep + self.near(given, 1)
        keep_near = self.near(keep, 2)
        first, early, cross = pl.pallas_call(
            functools.partial(ready_kernel, steps, per),
            out_shape=(
                jax.ShapeDtypeStruct((steps, block, targets.shape[1]), jnp.float32),
                jax.ShapeDtypeStruct((2, steps, begun * per, rows), jnp.bfloat16),
                jax.ShapeDtypeStruct((block, rows), jnp.float32),
            ),
            in_specs=[SMEM] + [VMEM] * 5,
            out_specs=(VMEM,) * 3,
            compiler_params=PARAMS,
            cost_estimate=cost(3 * steps * block * block, targets.shape[1]),
        )(self.place, first, self.near(first, 1), turned, gram, self.near(gram, 1))
        keep, first = hold((keep + keep_near, first))
        return [self.place, early, cross, keep, self.near(keep, 1)], first


class Gathers:
    def __init__(self):
        size = lax.axis_size("rows")
        self.order = (lax.axis_index("rows") + jnp.arange(size)) % size

    def turn(self, own):
        every = lax.all_gather(own, "rows", axis=0, tiled=True)
        start = lax.axis_index("rows") * own.shape[0]
        return lax.dynamic_slice_in_dim(
            jnp.concatenate([every, every], axis=0), start, every.shape[0], 0
        )

    def run(self, features, targets, block_index, turned, per):
        steps = block_index.shape[0]
        rank = lax.axis_index("rows")
        picks = lax.dynamic_slice_in_dim(block_index, rank * per, per, 1).reshape(-1)
        picks = picks - rank * features.shape[0]
        every = self.turn(jnp.take(features, picks, axis=0))
        width = targets.shape[1] // lax.axis_size("feat")
        start = lax.axis_index("feat") * width
        share = jnp.take(lax.dynamic_slice_in_dim(targets, start, width, 1), picks, axis=0)
        share = lax.all_gather(self.turn(share), "feat", axis=1, tiled=True)
        blocks = by_step(every, steps, per)
        cross = jnp.concatenate(
            [dot_rows(blocks[step], blocks[before]) for step, before in pairs_of(steps)], axis=1
        )
        gram, cross = lax.psum((dot_rows(every, features), cross), "feat")
        first = lax.dot_general(
            turned,
            by_step(share, steps, per),
            (((2,), (1,)), ((0,), (0,))),
            precision=lax.Precision.HIGHEST,
            preferred_element_type=jnp.float32,
        )
        return [gram, cross], first


def local(features, targets, block_index, inverse):
    rank = lax.axis_index("rows")
    row_count = lax.axis_size("rows")
    rows = features.shape[0]
    steps, block = block_index.shape
    per = block // row_count
    fits = rows == len(pairs_of(steps)) * block and per % 16 == 0 and features.shape[1] % (128 * PIECES) == 0
    lined = fits and (row_count, lax.axis_size("feat")) == (8, 4)
    mover = Lines() if lined else Gathers()

    place = jnp.arange(block)
    moved = jnp.repeat(mover.order, per) * per + place % per
    swap = moved[:, None] == place[None, :]
    picks = jnp.sum(jnp.where(swap[None], block_index[:, None, :], 0), axis=2)
    swap = swap.astype(jnp.float32)
    turned = jnp.stack([exact_dot(exact_dot(swap, inverse[step]), swap.T) for step in range(steps)])
    same = jnp.concatenate(
        [
            (picks[step][:, None] == picks[before][None, :]).astype(jnp.float32)
            for step, before in pairs_of(steps)
        ],
        axis=1,
    )
    own = picks[:, :per].reshape(-1, 1) - rank * rows

    sums, first = mover.run(features, targets, block_index, turned, per)
    operands = sums + [same, first, turned, own, targets]
    out = jax.ShapeDtypeStruct(targets.shape, jnp.float32)
    return pl.pallas_call(
        functools.partial(finish_kernel, steps, per, lined),
        out_shape=(out, out),
        in_specs=([SMEM] if lined else []) + [VMEM] * (len(operands) - lined),
        out_specs=(VMEM, VMEM),
        compiler_params=PARAMS,
        cost_estimate=cost(3 * rows * steps * block, targets.shape[1]),
    )(*operands)


def solution(mesh):
    return jax.shard_map(
        local,
        mesh=mesh,
        in_specs=(P("rows", "feat"), P("rows", None), P(), P()),
        out_specs=(P("rows", None), P("rows", None)),
        check_vma=False,
    )
```

```python
import functools

import jax
import jax.numpy as jnp
from jax import lax
from jax.experimental import pallas as pl
from jax.experimental.pallas import tpu as pltpu
from jax.sharding import PartitionSpec as P

F = 24576
VMEM = pl.BlockSpec(memory_space=pltpu.VMEM)
SMEM = pl.BlockSpec(memory_space=pltpu.SMEM)
HBM = pl.BlockSpec(memory_space=pltpu.HBM)
PIECES = 4
PARAMS = pltpu.CompilerParams(vmem_limit_bytes=24 * 1024 * 1024)
PICK = pltpu.CompilerParams(vmem_limit_bytes=58 * 1024 * 1024)
GRAM = pltpu.CompilerParams(vmem_limit_bytes=32 * 1024 * 1024)


def quadratic(gram):
    scaled = gram * (1.0 / F)
    return scaled + scaled * scaled


def dot_rows(left, right):
    return lax.dot_general(
        left, right, (((1,), (1,)), ((), ())), preferred_element_type=jnp.float32
    )


def exact_dot(left, right):
    return jnp.dot(
        left, right, precision=lax.Precision.HIGHEST, preferred_element_type=jnp.float32
    )


def split(array):
    high = array.astype(jnp.bfloat16)
    return high, (array - high.astype(jnp.float32)).astype(jnp.bfloat16)


def fine_dot(left, right, contract=1):
    sides = (((contract,), (0,)), ((), ()))
    left_high, left_low = left if isinstance(left, tuple) else split(left)
    right_high, right_low = right if isinstance(right, tuple) else split(right)

    def part(one, other):
        return lax.dot_general(one, other, sides, preferred_element_type=jnp.float32)

    return part(left_high, right_high) + (part(left_high, right_low) + part(left_low, right_high))


def pairs_of(steps):
    return [(step, before) for step in range(steps) for before in range(step)]


def of_step(slots, step, per):
    return jnp.concatenate([slot[step * per : (step + 1) * per] for slot in slots], axis=0)


def by_step(array, steps, per):
    parts = array.reshape(-1, steps, per, array.shape[-1])
    return jnp.swapaxes(parts, 0, 1).reshape(steps, -1, array.shape[-1])


def cost(rows, columns):
    return pl.CostEstimate(flops=2 * rows * columns, bytes_accessed=4 * rows, transcendentals=0)


def finish_kernel(steps, per, last, *refs):
    refs = list(refs)
    if last:
        place_ref, early_ref, cross_ref, mine_ref, other_ref = refs[:5]
        refs = refs[5:]
    else:
        gram_ref, cross_ref = refs[:2]
        refs = refs[2:]
    same_ref, first_ref, inverse_ref, own_ref, targets_ref, resid_ref, coeff_ref = refs
    block = first_ref.shape[1]
    rows = targets_ref.shape[0]
    if last:
        core = place_ref[1]
        mine, other = mine_ref[...], other_ref[...]
        end_gram = quadratic(jnp.where(core == 0, mine, other))
        end = jnp.where(core == 0, other, mine)
        count = steps * per
        begun = block - end.shape[0] // steps
        column = lax.broadcasted_iota(jnp.int32, (block, block), 0) < begun

        def end_of(array, step):
            slots = [array[i : i + count] for i in range(0, array.shape[0], count)]
            return of_step(slots, step, per)

        def of(one, other):
            part = end_of(end, one)[:, other * block : (other + 1) * block]
            return jnp.concatenate([jnp.zeros((begun, block), jnp.float32), part], axis=0)

    between = {}
    for at, (step, before) in enumerate(pairs_of(steps)):
        part = cross_ref[:, at * block : (at + 1) * block]
        if last:
            part = part + of(step, before) + jnp.where(column, of(before, step).T, 0.0)
        between[step, before] = split(quadratic(part) + same_ref[:, at * block : (at + 1) * block])
    deltas = []
    for step in range(steps):
        delta = first_ref[step]
        if step:
            change = fine_dot(between[step, 0], deltas[0])
            for before in range(1, step):
                change += fine_dot(between[step, before], deltas[before])
            delta = delta - fine_dot(inverse_ref[step], change)
        deltas.append(split(delta))
    spread = own_ref[...] == lax.broadcasted_iota(jnp.int32, (steps * per, rows), 1)
    spread = spread.astype(jnp.float32).astype(jnp.bfloat16)
    sides = (((0,), (0,)), ((), ()))
    coeffs = jnp.zeros(targets_ref.shape, jnp.float32)
    resid = targets_ref[...]
    for high_or_low in (0, 1):
        own = jnp.concatenate([delta[high_or_low][:per] for delta in deltas], axis=0)
        coeffs += lax.dot_general(spread, own, sides, preferred_element_type=jnp.float32)
    coeff_ref[...] = coeffs
    for step in range(steps):
        if last:
            part = split(end_of(end_gram, step))
            kernel = tuple(
                jnp.concatenate([early_ref[i, step], part[i]], axis=0) for i in range(2)
            )
        else:
            kernel = quadratic(gram_ref[...].reshape(-1, steps, per, rows)[:, step].reshape(block, rows))
        resid = resid - fine_dot(kernel, deltas[step], 0)
    resid_ref[...] = resid - coeffs


def ready_kernel(steps, per, place_ref, *refs):
    mine_ref, other_ref, inverse_ref, *gram_refs, first_ref, early_ref, cross_ref = refs
    core = place_ref[1]
    block = inverse_ref.shape[1]
    half = mine_ref.shape[1]
    for step in range(steps):
        rows = slice(step * block, (step + 1) * block)
        inverse = split(inverse_ref[step])
        mine, other = mine_ref[rows], other_ref[rows]
        first_ref[step, :, :half] = fine_dot(inverse, jnp.where(core == 0, mine, other))
        first_ref[step, :, half:] = fine_dot(inverse, jnp.where(core == 0, other, mine))
    mine, other = gram_refs[0][...], gram_refs[1][...]
    gram = jnp.concatenate([jnp.where(core == 0, mine, other), jnp.where(core == 0, other, mine)], axis=0)
    cross_ref[...] = gram[-block:]
    kernel = quadratic(gram[:-block])
    kernel = kernel.reshape(-1, steps, per, kernel.shape[-1])
    for step in range(steps):
        early_ref[0, step], early_ref[1, step] = split(kernel[:, step].reshape(early_ref.shape[2:]))


def pieces_of(features_ref):
    width = features_ref.shape[1] // PIECES
    return [slice(i * width, (i + 1) * width) for i in range(PIECES)]


def fetch(features_ref, held_ref, sems):
    copies = []
    for i, at in enumerate(pieces_of(features_ref)):
        copies.append(pltpu.make_async_copy(features_ref.at[:, at], held_ref.at[:, at], sems.at[i]))
        copies[-1].start()
    return copies


def held(features):
    return [pltpu.VMEM(features.shape, features.dtype), pltpu.SemaphoreType.DMA((PIECES,))]


def add(total, part):
    return part if total is None else total + part


def pick_kernel(
    per, index_hbm, features_ref, targets_ref, out_ref, index_ref, held_targets, side_sems, held_ref, sems
):
    index = pltpu.make_async_copy(index_hbm, index_ref, side_sems.at[0])
    index.start()
    copies = fetch(features_ref, held_ref, sems)
    side = pltpu.make_async_copy(targets_ref, held_targets, side_sems.at[1])
    side.start()
    index.wait()
    rank, core = lax.axis_index("rows"), lax.rem(lax.axis_index("feat"), 2)
    rows, columns = features_ref.shape
    steps = index_ref.shape[0]
    line = lax.broadcasted_iota(jnp.int32, (steps * per, 128), 0)
    wanted = jnp.zeros((steps * per, 128), jnp.int32)
    for step in range(steps):
        for i in range(per):
            wanted = jnp.where(line == step * per + i, index_ref[step, rank * per + i], wanted)
    chosen = wanted[:, :1] - rank * rows == lax.broadcasted_iota(jnp.int32, (steps * per, rows), 1)
    chosen = chosen.astype(jnp.float32).astype(jnp.bfloat16)

    def take(array):
        return jnp.dot(chosen, array, preferred_element_type=jnp.float32).astype(jnp.bfloat16)

    for copy, at in zip(copies, pieces_of(features_ref)):
        copy.wait()
        out_ref[:, at] = take(held_ref[:, at])
    side.wait()
    width = targets_ref.shape[1] // 2
    values = jnp.where(core == 0, held_targets[:, :width], held_targets[:, width:])
    high, low = split(values)
    out_ref[:, columns : columns + width] = take(high)
    out_ref[:, columns + width :] = take(low)


def pick(block_index, features, targets, per):
    count = block_index.shape[0] * per
    wide = features.shape[1] + targets.shape[1]
    return pl.pallas_call(
        functools.partial(pick_kernel, per),
        out_shape=jax.ShapeDtypeStruct((count, wide), features.dtype),
        in_specs=[HBM, HBM, HBM],
        out_specs=VMEM,
        scratch_shapes=[
            pltpu.SMEM(block_index.shape, jnp.int32),
            pltpu.VMEM(targets.shape, jnp.float32),
            pltpu.SemaphoreType.DMA((2,)),
        ]
        + held(features),
        compiler_params=PICK,
        cost_estimate=cost(count * features.shape[0], wide),
    )(block_index, features, targets)


def gram_kernel(steps, per, missing, place_ref, *refs):
    *slot_refs, features_ref, keep_ref, send_ref = refs
    total = [None] * (1 + len(pairs_of(steps)))
    for at in pieces_of(features_ref):
        slots = [ref[:, at] for ref in slot_refs]
        slots += [jnp.zeros_like(slots[0])] * missing
        rows = [of_step(slots, step, per) for step in range(steps)]
        for i, (step, before) in enumerate(pairs_of(steps)):
            total[1 + i] = add(total[1 + i], dot_rows(rows[step], rows[before]))
    for at in pieces_of(features_ref):
        slots = jnp.concatenate([ref[:, at] for ref in slot_refs], axis=0)
        total[0] = add(total[0], dot_rows(slots, features_ref[:, at]))
    total = jnp.concatenate([total[0], jnp.concatenate(total[1:], axis=1)], axis=0)
    half = keep_ref.shape[0]
    core = place_ref[1]
    keep_ref[...] = jnp.where(core == 0, total[:half], total[half:])
    send_ref[...] = jnp.where(core == 0, total[half:], total[:half])


def last_kernel(steps, per, begun, place_ref, *refs):
    *slot_refs, inner_ref, left_ref, right_ref, features_ref = refs[:-3]
    keep_ref, send_ref, first_ref = refs[-3:]
    core = place_ref[1]
    inner = place_ref[2] == 1
    columns = features_ref.shape[1]

    def slots_at(at):
        slots = [ref[:, at] for ref in slot_refs]
        other = slots.pop()
        slots[-1] = jnp.where(inner, slots[-1], other)
        last = jnp.where(core == 0, left_ref[:, at], right_ref[:, at])
        return slots + [jnp.where(inner, inner_ref[:, at], last)]

    def every(slots):
        return jnp.concatenate([of_step(slots, step, per) for step in range(steps)], axis=0)

    total, cross = None, None
    for at in pieces_of(features_ref):
        slots = slots_at(at)
        cross = add(cross, dot_rows(every(slots), jnp.concatenate(slots[begun:], axis=0)))
    for at in pieces_of(features_ref):
        new = jnp.concatenate(slots_at(at)[begun:], axis=0)
        total = add(total, dot_rows(features_ref[:, at], new))
    total, cross = total.T, cross.T
    keep_ref[...] = jnp.where(core == 0, total, cross)
    send_ref[...] = jnp.where(core == 0, cross, total)
    width = (inner_ref.shape[1] - columns) // 2
    high = every(slots_at(slice(columns, columns + width)))
    low = every(slots_at(slice(columns + width, columns + 2 * width)))
    first_ref[...] = high.astype(jnp.float32) + low.astype(jnp.float32)


class Lines:
    def __init__(self):
        self.beside = [(r, r ^ 1) for r in range(8)]
        self.pair = [(r, r ^ 2) for r in range(8)]
        self.inner = [(r, r ^ 6) for r in range(2, 6)]
        self.outer = [(2, 0), (3, 1), (4, 6), (5, 7)]
        ends = [(r, r ^ 1) for r in (0, 1, 6, 7)]
        self.ends = [(4 * r + f, 4 * to + f) for r, to in ends for f in (0, 2)]
        self.outer_second = [(4 * r + f, 4 * to + f) for r, to in self.outer for f in (1, 3)]
        rank = lax.axis_index("rows")
        core = lax.axis_index("feat") % 2
        self.is_inner = (rank >= 2) & (rank < 6)
        self.order = rank ^ jnp.arange(8)
        self.place = jnp.stack([rank, core, self.is_inner.astype(jnp.int32)])

    def near(self, array, bit):
        return lax.ppermute(array, "feat", [(f, f ^ bit) for f in range(4)])

    def send(self, array, pairs):
        return lax.ppermute(array, "rows", pairs)

    def run(self, features, targets, block_index, turned, per):
        rows, columns = features.shape
        steps, block = block_index.shape
        count = steps * per
        hold = lax.optimization_barrier
        own = pick(block_index, features, targets, per)

        pair = self.send(own, self.pair)
        mid = self.send(own, self.inner)
        own_b = self.send(own, self.beside)
        pair, own_b = hold((pair, own_b))

        far = self.send(pair, self.inner)
        mid_end = self.send(mid, self.outer)
        pair_b = self.send(pair, self.beside)
        far, pair_b, own_b = hold((far, pair_b, own_b))

        far_end = self.send(far, self.outer)
        third = jnp.where(self.is_inner, far, mid_end)
        third_b = self.send(third, self.beside)
        last_in = self.send(own_b, self.inner)
        slots = [own, own_b, pair, pair_b, third]
        begun = len(slots)
        part = jax.ShapeDtypeStruct(((begun * count + block) // 2, rows), jnp.float32)
        gram, given = pl.pallas_call(
            functools.partial(gram_kernel, steps, per, 8 - begun),
            out_shape=(part, part),
            in_specs=[SMEM] + [VMEM] * begun + [VMEM],
            out_specs=(VMEM, VMEM),
            compiler_params=GRAM,
            cost_estimate=cost((begun * count + block) * rows, columns),
        )(self.place, *slots, features)
        gram = gram + self.near(given, 1)
        third_b, far_end, last_in, gram = hold((third_b, far_end, last_in, gram))

        left = lax.ppermute(far_end, ("rows", "feat"), self.ends)
        right = lax.ppermute(third_b, ("rows", "feat"), self.outer_second)
        gram_near = self.near(gram, 2)
        left, right, gram_near = hold((left, right, gram_near))
        gram = gram + gram_near

        slots = slots + [third_b, mid, far_end, last_in, left, right]
        end = jax.ShapeDtypeStruct(((8 - begun) * count, rows), jnp.float32)
        keep, given, first = pl.pallas_call(
            functools.partial(last_kernel, steps, per, begun),
            out_shape=(
                end,
                end,
                jax.ShapeDtypeStruct((steps * block, targets.shape[1] // 2), jnp.float32),
            ),
            in_specs=[SMEM] + [VMEM] * len(slots) + [VMEM],
            out_specs=(VMEM,) * 3,
            compiler_params=GRAM,
            cost_estimate=cost((8 - begun) * count * (rows + steps * block), columns),
        )(self.place, *slots, features)
        keep = keep + self.near(given, 1)
        keep_near = self.near(keep, 2)
        first, early, cross = pl.pallas_call(
            functools.partial(ready_kernel, steps, per),
            out_shape=(
                jax.ShapeDtypeStruct((steps, block, targets.shape[1]), jnp.float32),
                jax.ShapeDtypeStruct((2, steps, begun * per, rows), jnp.bfloat16),
                jax.ShapeDtypeStruct((block, rows), jnp.float32),
            ),
            in_specs=[SMEM] + [VMEM] * 5,
            out_specs=(VMEM,) * 3,
            compiler_params=PARAMS,
            cost_estimate=cost(3 * steps * block * block, targets.shape[1]),
        )(self.place, first, self.near(first, 1), turned, gram, self.near(gram, 1))
        keep, first = hold((keep + keep_near, first))
        return [self.place, early, cross, keep, self.near(keep, 1)], first


class Gathers:
    def __init__(self):
        size = lax.axis_size("rows")
        self.order = (lax.axis_index("rows") + jnp.arange(size)) % size

    def turn(self, own):
        every = lax.all_gather(own, "rows", axis=0, tiled=True)
        start = lax.axis_index("rows") * own.shape[0]
        return lax.dynamic_slice_in_dim(
            jnp.concatenate([every, every], axis=0), start, every.shape[0], 0
        )

    def run(self, features, targets, block_index, turned, per):
        steps = block_index.shape[0]
        rank = lax.axis_index("rows")
        picks = lax.dynamic_slice_in_dim(block_index, rank * per, per, 1).reshape(-1)
        picks = picks - rank * features.shape[0]
        every = self.turn(jnp.take(features, picks, axis=0))
        width = targets.shape[1] // lax.axis_size("feat")
        start = lax.axis_index("feat") * width
        share = jnp.take(lax.dynamic_slice_in_dim(targets, start, width, 1), picks, axis=0)
        share = lax.all_gather(self.turn(share), "feat", axis=1, tiled=True)
        blocks = by_step(every, steps, per)
        cross = jnp.concatenate(
            [dot_rows(blocks[step], blocks[before]) for step, before in pairs_of(steps)], axis=1
        )
        gram, cross = lax.psum((dot_rows(every, features), cross), "feat")
        first = lax.dot_general(
            turned,
            by_step(share, steps, per),
            (((2,), (1,)), ((0,), (0,))),
            precision=lax.Precision.HIGHEST,
            preferred_element_type=jnp.float32,
        )
        return [gram, cross], first


def local(features, targets, block_index, inverse):
    rank = lax.axis_index("rows")
    row_count = lax.axis_size("rows")
    rows = features.shape[0]
    steps, block = block_index.shape
    per = block // row_count
    fits = rows == len(pairs_of(steps)) * block and per % 16 == 0 and features.shape[1] % (128 * PIECES) == 0
    lined = fits and (row_count, lax.axis_size("feat")) == (8, 4)
    mover = Lines() if lined else Gathers()

    place = jnp.arange(block)
    moved = jnp.repeat(mover.order, per) * per + place % per
    swap = moved[:, None] == place[None, :]
    picks = jnp.sum(jnp.where(swap[None], block_index[:, None, :], 0), axis=2)
    swap = swap.astype(jnp.float32)
    turned = jnp.stack([exact_dot(exact_dot(swap, inverse[step]), swap.T) for step in range(steps)])
    same = jnp.concatenate(
        [
            (picks[step][:, None] == picks[before][None, :]).astype(jnp.float32)
            for step, before in pairs_of(steps)
        ],
        axis=1,
    )
    own = picks[:, :per].reshape(-1, 1) - rank * rows

    sums, first = mover.run(features, targets, block_index, turned, per)
    operands = sums + [same, first, turned, own, targets]
    out = jax.ShapeDtypeStruct(targets.shape, jnp.float32)
    return pl.pallas_call(
        functools.partial(finish_kernel, steps, per, lined),
        out_shape=(out, out),
        in_specs=([SMEM] if lined else []) + [VMEM] * (len(operands) - lined),
        out_specs=(VMEM, VMEM),
        compiler_params=PARAMS,
        cost_estimate=cost(3 * rows * steps * block, targets.shape[1]),
    )(*operands)


def solution(mesh):
    return jax.shard_map(
        local,
        mesh=mesh,
        in_specs=(P("rows", "feat"), P("rows", None), P(), P()),
        out_specs=(P("rows", None), P("rows", None)),
        check_vma=False,
    )
```
